128 devices in a mesh: lat: 8 (over x_lo, y), lon: 16 (over z, x_hi, core).
Axes of the slice: x: 4 (x_hi: 2, x_lo: 2; x = x_hi * 2 + x_lo), y: 4, z: 4, core: 2. Of those that a mesh axis runs over, the one named last changes fastest.
Arguments:
- records: bfloat16 [128, 128, 1024], P(('lat', 'lon')), may hold values from -6 to 6
- cell_ids: int32 [128, 128, 16], P(('lat', 'lon')), may hold values from 0 to 767
- counts: int32 [128, 128], P(('lat', 'lon')), may hold values from 0 to 16, as said below
- embed: bfloat16 [64, 256], replicated, may hold values from -0.75 to 0.75
- kernels: bfloat16 [3, 3, 3, 256, 256], replicated, may hold values from -0.125 to 0.125
- down: bfloat16 [2, 2, 256, 256], replicated, may hold values from -0.1875 to 0.1875
- cotangent: bfloat16 [64, 384, 256], P('lat', 'lon'), may hold values from -6 to 6
Outputs:
- coarse: bfloat16 [64, 384, 256], P('lat', 'lon')
- kernel_update: bfloat16 [3, 3, 3, 256, 256], replicated
- down_update: bfloat16 [2, 2, 256, 256], replicated
- embed_update: bfloat16 [64, 256], replicated
The draws below stay inside these ranges and needn't reach their ends.
Inputs may be any that keep to these rules, and one draw needn't show every extreme that they name: counts[s, d] slots of the 16 from tile s to tile d are live, the first ones; the others carry records that no output reads. Every tile sends 16 records to itself, and some tile receives 16 from every tile.
All inputs are finite; a program needn't handle non-finite values.
Results may differ from the reference program's by a relative error of at most 0.015.
Values may be sent and summed in bfloat16 or wider, within the bound.
A program may use at most 128 MiB of HBM per device.

```python
import jax
import jax.numpy as jnp
from jax import lax

C = 256
V = 64
LAYERS = 3
TH = 16
TW = 48
CAP = 16
TILES = 128
NH = 128
NW = 768
N_LON = 16


def draw_counts(key, part):
    first_key, second_key, third_key = jax.random.split(key, 3)
    base = jax.random.randint(first_key, (TILES, TILES), 0, CAP + 1)
    density = jax.random.randint(second_key, (1, TILES), 1, 5)
    filled = jnp.minimum(CAP, base * density // 2)
    hotspot = jax.random.randint(third_key, (), 0, TILES)
    column = jnp.arange(TILES)[None, :]
    row_index = jnp.arange(TILES)[:, None]
    filled = jnp.where((column == hotspot) | (column == row_index), CAP, filled)
    return filled.astype(jnp.int32)


def touch_ends(array, key, smallest, high):
    dims = array.shape
    spot = [jax.random.randint(jax.random.fold_in(key, axis), (), 0, dims[axis]) for axis in range(len(dims))]
    array = array.at[tuple(spot)].set(smallest)
    longest = dims.index(max(dims))
    spot[longest] = (spot[longest] + 1) % dims[longest]
    return array.at[tuple(spot)].set(high)


def block_levels(own_key, extent, cuts, smallest, largest):
    def one(dim, shards_of):
        draws = jax.random.uniform(jax.random.fold_in(jax.random.fold_in(own_key, 6), dim), (shards_of,), jnp.float32, smallest / len(cuts), largest / len(cuts))
        return jnp.repeat(jnp.exp(draws), extent[dim] // shards_of).reshape((-1,) + (1,) * (len(extent) - dim - 1))

    factor_of = one(*cuts[0])
    for cut in cuts[1:]:
        factor_of = factor_of * one(*cut)
    return factor_of


def gaussian(own_key, dims, deviation, limit, cuts=(), kind=jnp.bfloat16):
    values = jax.random.normal(own_key, dims, jnp.float32) * deviation
    if len(cuts) > 0:
        values = block_levels(own_key, dims, cuts, -0.22, 0.18) * values
    return jnp.clip(values, min=-limit, max=limit).astype(kind)


def setup_inputs(seed: int = 0) -> dict:
    key_list = jax.random.split(jax.random.key(seed), 8)
    records = gaussian(key_list[0], (TILES, TILES, CAP * V), 1.0, 6.0, ((0, 128),))
    cell_ids = touch_ends(jax.random.randint(key_list[1], (TILES, TILES, CAP), 0, TH * TW), jax.random.fold_in(key_list[1], 1), 0, (TH * TW) - 1).astype(jnp.int32)
    counts = draw_counts(jax.random.fold_in(key_list[7], 71), 0)
    embed = gaussian(key_list[3], (V, C), V ** -0.5, 0.75)
    kernels = gaussian(key_list[4], (LAYERS, 3, 3, C, C), (9 * C) ** -0.5, 0.125)
    down = gaussian(key_list[5], (2, 2, C, C), (4 * C) ** -0.5, 0.1875)
    cotangent = gaussian(key_list[6], (NH // 2, NW // 2, C), 1.0, 6.0, ((0, 8), (1, 16)))
    return dict(records=records, cell_ids=cell_ids, counts=counts, embed=embed, kernels=kernels, down=down, cotangent=cotangent)


def pad_grid(field, rim):
    wrapped = jnp.concatenate([field[:, -rim:], field, field[:, :rim]], axis=1)
    return jnp.pad(wrapped, ((rim, rim), (0, 0), (0, 0)))

def conv_grid(padded, kernel):
    height = padded.shape[0] - 2
    breadth = padded.shape[1] - 2
    summed = jnp.zeros((height, breadth, kernel.shape[3]), jnp.float32)
    for row_shift in range(3):
        for col_shift in range(3):
            window = padded[row_shift:row_shift + height, col_shift:col_shift + breadth].astype(jnp.float32)
            summed = summed + jnp.einsum('hwc,cd->hwd', window, kernel[row_shift, col_shift].astype(jnp.float32))
    return summed

def conv_back(padded, kernel):
    height = padded.shape[0] - 2
    breadth = padded.shape[1] - 2
    summed = jnp.zeros((height, breadth, kernel.shape[2]), jnp.float32)
    for row_shift in range(3):
        for col_shift in range(3):
            window = padded[2 - row_shift:2 - row_shift + height, 2 - col_shift:2 - col_shift + breadth].astype(jnp.float32)
            summed = summed + jnp.einsum('hwd,cd->hwc', window, kernel[row_shift, col_shift].astype(jnp.float32))
    return summed

def kernel_grad(padded, dgrad):
    height = dgrad.shape[0]
    breadth = dgrad.shape[1]
    grad_float = dgrad.astype(jnp.float32)
    rows_out = []
    for row_shift in range(3):
        cols_out = []
        for col_shift in range(3):
            window = padded[row_shift:row_shift + height, col_shift:col_shift + breadth].astype(jnp.float32)
            cols_out.append(jnp.einsum('hwc,hwd->cd', window, grad_float))
        rows_out.append(jnp.stack(cols_out, 0))
    return jnp.stack(rows_out, 0)

def reference(records, cell_ids, counts, embed, kernels, down, cotangent):
    channels = embed.shape[1]
    obs_width = embed.shape[0]
    dest = jnp.arange(TILES, dtype=jnp.int32)[None, :, None]
    lat_row = dest // N_LON * TH + cell_ids // TW
    lon_col = dest % N_LON * TW + cell_ids % TW
    flat_cell = (lat_row * NW + lon_col).reshape(-1).astype(jnp.int32)
    live = (jnp.arange(CAP, dtype=jnp.int32)[None, None, :] < counts[:, :, None]).reshape(-1)
    values = records.reshape(TILES * TILES * CAP, obs_width).astype(jnp.float32) * live[:, None].astype(jnp.float32)
    cell_sum = jax.ops.segment_sum(values, flat_cell, num_segments=NH * NW)
    tally = jax.ops.segment_sum(live.astype(jnp.float32), flat_cell, num_segments=NH * NW)
    mean_obs = (cell_sum / jnp.maximum(tally, 1.0)[:, None]).astype(jnp.bfloat16)
    current = jnp.dot(mean_obs, embed, preferred_element_type=jnp.float32).astype(jnp.bfloat16).reshape(NH, NW, channels)
    saved_inputs = []
    saved_pre = []
    for layer_number in range(LAYERS):
        padded = pad_grid(current, 1)
        pre = conv_grid(padded, kernels[layer_number])
        saved_inputs.append(padded)
        saved_pre.append(pre)
        current = (current.astype(jnp.float32) + jax.nn.silu(pre)).astype(jnp.bfloat16)
    cot_float = cotangent.astype(jnp.float32)
    coarse_sum = jnp.zeros((NH // 2, NW // 2, channels), jnp.float32)
    down_rows = []
    back_rows = []
    for row_shift in range(2):
        down_cols = []
        back_cols = []
        for col_shift in range(2):
            piece = current[row_shift::2, col_shift::2].astype(jnp.float32)
            weight = down[row_shift, col_shift].astype(jnp.float32)
            coarse_sum = coarse_sum + jnp.einsum('hwc,cd->hwd', piece, weight)
            down_cols.append(jnp.einsum('hwc,hwd->cd', piece, cot_float))
            back_cols.append(jnp.einsum('hwd,cd->hwc', cot_float, weight))
        down_rows.append(jnp.stack(down_cols, 0))
        back_rows.append(jnp.stack(back_cols, axis=2))
    coarse = coarse_sum.astype(jnp.bfloat16)
    grad_down = jnp.stack(down_rows, 0)
    upstream = jnp.stack(back_rows, axis=1).reshape(NH, NW, channels)
    grads = [None] * LAYERS
    for layer_number in reversed(range(LAYERS)):
        pre = saved_pre[layer_number]
        sig = jax.nn.sigmoid(pre)
        dgrad = (upstream * sig * (1.0 + pre * (1.0 - sig))).astype(jnp.bfloat16)
        grads[layer_number] = kernel_grad(saved_inputs[layer_number], dgrad)
        upstream = upstream + conv_back(pad_grid(dgrad, 1), kernels[layer_number])
    grad_kernels = jnp.stack(grads, 0)
    upstream_round = upstream.astype(jnp.bfloat16).reshape(NH * NW, channels)
    grad_embed = lax.dot_general(mean_obs, upstream_round, (((0,), (0,)), ((), ())), preferred_element_type=jnp.float32)
    squares = jnp.sum(grad_kernels * grad_kernels) + jnp.sum(grad_down * grad_down) + jnp.sum(grad_embed * grad_embed)
    entries = (LAYERS * 9 + 4) * channels * channels + obs_width * channels
    norm_scale = 1.0 / jnp.sqrt(squares / entries + 1e-06)
    return (coarse, (grad_kernels * norm_scale).astype(jnp.bfloat16), (grad_down * norm_scale).astype(jnp.bfloat16), (grad_embed * norm_scale).astype(jnp.bfloat16))
```

```python
import jax
import jax.numpy as jnp
from jax import lax
from jax.experimental import pallas as pl
from jax.experimental.pallas import tpu as pltpu
from jax.sharding import PartitionSpec as P

F32 = jnp.float32
BF16 = jnp.bfloat16
MESH = pl.DeviceIdType.MESH

ROWS, WIDE = 28, 64
PIECES = ((0, 1, 2), (3, 4), (5, 6, 7))
GROUPS = ((0, 3, 5), (1, 4, 6), (2, 7))
GROUP_OF = {u: g for g, us in enumerate(GROUPS) for u in us}
PLACE = {u: g * 3 + i for g, us in enumerate(GROUPS) for i, u in enumerate(us)}


def nn(a, b):
    return jnp.dot(a, b, preferred_element_type=F32)


def nt(a, b):
    return lax.dot_general(a, b, (((1,), (1,)), ((), ())), preferred_element_type=F32)


def body(
    values_ref, ids_ref, idst_ref, embed_ref, kern_ref, down_ref, cot_ref,
    coarse_ref, kup_ref, dup_ref, eup_ref,
    onehot, spread, mean, cpad, fine_e, fine_o, eo, up, x3, fac, dy3, dym, xt, xl, ybuf,
    grad, core_in, acc1, in1, acc2, in2, acc3, in3, gath,
    halo_s, halo_r, rs_s, rs_r, ag_s, ag_r,
):
    lat = lax.axis_index("lat")
    lon = lax.axis_index("lon")
    xx = lax.rem(lon // 2, 2) * 2 + lat // 4
    yy = lax.rem(lat, 4)
    zz = lon // 4
    core = lax.rem(lon, 2)
    pos = (xx, yy, zz)

    def at(axis, k):
        c = list(pos)
        c[axis] = lax.rem(c[axis] + k, 4)
        return (lax.rem(c[0], 2) * 4 + c[1], c[2] * 4 + (c[0] // 2) * 2 + core)

    other = (lat, lon + 1 - 2 * core)

    def side(dr, dc):
        return (lax.rem(lat + dr + 8, 8), lax.rem(lon + dc + 16, 16))

    sides = [(r, c) for r in (-1, 0, 1) for c in (-1, 0, 1) if (r, c) != (0, 0)]
    partners = [side(r, c) for r, c in sides] + [other]
    partners += [at(a, k) for a in range(3) for k in (1, 2, 3)]
    barrier = pltpu.get_barrier_semaphore()
    for who in partners:
        pl.semaphore_signal(barrier, inc=1, device_id=who, device_id_type=MESH)

    cpad[2:10, 8:32, :] = cot_ref[...].astype(F32)
    pl.semaphore_wait(barrier, len(partners))

    def span(step, rows, lead, cols, near):
        if step[0] == 0:
            r_src = r_dst = (lead, rows)
        elif step[0] < 0:
            r_src, r_dst = (lead, lead), (lead + rows, lead)
        else:
            r_src, r_dst = (rows, lead), (0, lead)
        if step[1] == 0:
            c_src = c_dst = (8, cols)
        elif step[1] < 0:
            c_src, c_dst = (8, 8), (8 + cols, 8)
        else:
            c_src, c_dst = (cols, 8), (0, 8)
        return r_src, c_src, r_dst, c_dst

    def halo(ref, rows, lead, cols, which):
        copies = []
        for n, step in enumerate(sides):
            (a, la), (b, lb), (c, lc), (d, ld) = span(step, rows, lead, cols, None)
            copies.append(
                pltpu.make_async_remote_copy(
                    src_ref=ref.at[pl.ds(a, la), pl.ds(b, lb), :],
                    dst_ref=ref.at[pl.ds(c, lc), pl.ds(d, ld), :],
                    send_sem=halo_s.at[which, n],
                    recv_sem=halo_r.at[which, n],
                    device_id=side(*step),
                    device_id_type=MESH,
                )
            )
        for c in copies:
            c.start()
        return copies

    cot_copies = halo(cpad, 8, 2, 24, 0)

    cells = lax.broadcasted_iota(jnp.int32, (384, 128), 0)
    low = lax.broadcasted_iota(jnp.int32, (128, 128), 1) < 64
    for k in range(16):
        idr = idst_ref[k : k + 1, :]
        row = (idr * 1366) >> 16
        place = (row >> 1) * 48 + (idr - row * 48)
        place = jnp.where(idr < 0, -1, place)
        onehot[:, k * 128 : (k + 1) * 128] = jnp.where(cells == place, 1.0, 0.0).astype(BF16)
        idc = ids_ref[:, k : k + 1]
        par = ((idc * 1366) >> 16) & 1
        even = jnp.where((idc >= 0) & (par == 0), 1.0, 0.0)
        odd = jnp.where((idc >= 0) & (par == 1), 1.0, 0.0)
        flag = jnp.where(low, even, odd)
        pair = values_ref[:, (k // 2) * 128 : (k // 2 + 1) * 128].astype(F32)
        swap = pltpu.roll(pair, 64, 1)
        both = jnp.where(low, pair, swap) if k % 2 == 0 else jnp.where(low, swap, pair)
        spread[k * 128 : (k + 1) * 128, 0:128] = (both * flag).astype(BF16)
        spread[k * 128 : (k + 1) * 128, 128:256] = flag.astype(BF16)
    sums = nn(onehot[...], spread[...])
    means = (sums[:, 0:128] / jnp.maximum(sums[:, 128:256], 1.0)).astype(BF16).astype(F32)
    mean[3:11, 8:56, :] = means.reshape(8, 48, 128)
    mean_copies = halo(mean, 8, 3, 48, 1)

    for c in cot_copies:
        c.wait_recv()
    fine_e[...] = jnp.zeros_like(fine_e)
    fine_o[...] = jnp.zeros_like(fine_o)
    coarse_cells = cpad[:, 4:36, :].reshape(384, 256)
    for h in range(2):
        part = coarse_cells[:, h * 128 : (h + 1) * 128]
        fine_e[h, pl.ds(0, 384, stride=2), :] = part
        fine_o[h, pl.ds(1, 384, stride=2), :] = part
    for h in range(2):
        eo[:, :, h * 128 : (h + 1) * 128] = fine_e[h].astype(BF16).reshape(12, WIDE, 128)
        eo[:, :, 256 + h * 128 : 256 + (h + 1) * 128] = fine_o[h].astype(BF16).reshape(12, WIDE, 128)
    for a in range(2):
        flat = eo[...].reshape(12 * WIDE, 512)
        top = nt(flat[:, 0:256], down_ref[a, 0]) + nt(flat[:, 256:512], down_ref[a, 1])
        top = top.reshape(12, WIDE, 256)
        for i in range(12):
            up[2 * i + a] = top[i]

    def inside(first, count):
        row = lax.broadcasted_iota(jnp.int32, (count, 1, 1), 0) + (lat * 16 - 6 + first)
        return jnp.where((row >= 0) & (row < 128), 1.0, 0.0)

    column = lax.broadcasted_iota(jnp.int32, (1, WIDE, 1), 1)
    in_tile = jnp.where((column >= 8) & (column < 56), 1.0, 0.0)

    def store3(ref, first, count, value, order):
        flat = value.reshape(count * WIDE, 256)
        prev = pltpu.roll(flat, 1, 0)
        nxt = pltpu.roll(flat, count * WIDE - 1, 0)
        parts = (prev, flat, nxt) if order > 0 else (nxt, flat, prev)
        for b, part in enumerate(parts):
            ref[first : first + count, :, b * 256 : (b + 1) * 256] = part.astype(BF16).reshape(count, WIDE, 256)

    def turn(ref_slice, count):
        return ref_slice.reshape(count * WIDE, 256).T

    for c in mean_copies:
        c.wait_recv()
    for first in (0, 7):
        lhs = mean[first : first + 7].reshape(7 * WIDE, 128).astype(BF16)
        zero = jnp.zeros((64, 256), BF16)
        for par in range(2):
            both = (embed_ref[...], zero) if par == 0 else (zero, embed_ref[...])
            x0 = nn(lhs, jnp.concatenate(both, 0)).reshape(7, WIDE, 256)
            row = lax.broadcasted_iota(jnp.int32, (7, 1, 1), 0) * 2 + (lat * 16 - 6 + 2 * first + par)
            x0 = x0 * jnp.where((row >= 0) & (row < 128), 1.0, 0.0)
            flat = x0.reshape(7 * WIDE, 256)
            parts = (pltpu.roll(flat, 1, 0), flat, pltpu.roll(flat, 7 * WIDE - 1, 0))
            for b, part in enumerate(parts):
                part = part.astype(BF16).reshape(7, WIDE, 256)
                for i in range(7):
                    x3[0, 2 * (first + i) + par, :, b * 256 : (b + 1) * 256] = part[i]

    for l in range(3):
        first, count = l + 1, 26 - 2 * l
        half = count // 2
        for start in (first, first + half):
            y = jnp.zeros((half * WIDE, 256), F32)
            for a in range(3):
                y = y + nn(
                    x3[l, start + a - 1 : start + a - 1 + half].reshape(half * WIDE, 768),
                    kern_ref[l, a].reshape(768, 256),
                )
            s = jax.nn.sigmoid(y)
            gain = (s * (1.0 + y * (1.0 - s))).reshape(half, WIDE, 256)
            keep = inside(start, half)
            fac[l, start : start + half] = gain * keep
            x = x3[l, start : start + half, :, 256:512].reshape(half * WIDE, 256).astype(F32)
            x = (x + y * s).reshape(half, WIDE, 256)
            if l < 2:
                store3(x3.at[l + 1], start, half, x * keep, 1)
            else:
                xl[start : start + half] = (x * in_tile).astype(BF16)

    sum0 = jnp.zeros((512, 256), F32)
    sum1 = jnp.zeros((512, 256), F32)
    last = xl[6:22].reshape(8, 2, WIDE, 256)
    rights = eo[2:10].reshape(512, 512)
    for a in range(2):
        piece = last[:, a].reshape(512, 256)
        sum0 = sum0 + nn(piece, down_ref[a, 0])
        sum1 = sum1 + nn(piece, down_ref[a, 1])
        g = nn(piece.T, rights).astype(BF16)
        for b in range(2):
            for e in range(2):
                grad[e, 2 * a + b] = g[:, b * 256 + e * 128 : b * 256 + (e + 1) * 128]
    total = sum0 + pltpu.roll(sum1, 511, 0)
    for h in range(2):
        ybuf[h] = total[:, h * 128 : (h + 1) * 128]
    for h in range(2):
        picked = ybuf[h, pl.ds(0, 256, stride=2), :].reshape(8, 32, 128)
        coarse_ref[:, :, h * 128 : (h + 1) * 128] = picked[:, 4:28].astype(BF16)

    copies = {}

    def send(key, src, dst, who, sems, index):
        c = pltpu.make_async_remote_copy(
            src_ref=src, dst_ref=dst, send_sem=sems[0].at[index], recv_sem=sems[1].at[index],
            device_id=who, device_id_type=MESH,
        )
        c.start()
        copies[key] = c

    rs = (rs_s, rs_r)
    ag = (ag_s, ag_r)

    def give_core(piece):
        b0, n = 4 * PIECES[piece][0], 4 * len(PIECES[piece])
        send(
            ("c", piece), grad.at[1 - core, pl.ds(b0, n)], core_in.at[pl.ds(b0, n)], other, rs, 72 + piece
        )

    def step1(piece):
        copies["c", piece].wait_recv()
        for u in PIECES[piece]:
            for p in range(4):
                acc1[4 * u + p] = (grad[core, 4 * u + p].astype(F32) + core_in[4 * u + p].astype(F32)).astype(BF16)
            axis = GROUP_OF[u]
            for k in (1, 2, 3):
                p = lax.rem(pos[axis] + k, 4)
                send(("1", u, k), acc1.at[4 * u + p], in1.at[u, k - 1], at(axis, k), rs, u * 9 + k - 1)

    def step2(u):
        axis, nxt = GROUP_OF[u], (GROUP_OF[u] + 1) % 3
        for k in (1, 2, 3):
            copies["1", u, k].wait_recv()
        s = acc1[4 * u + pos[axis]].astype(F32)
        for k in range(3):
            s = s + in1[u, k].astype(F32)
        acc2[u] = s.astype(BF16)
        for k in (1, 2, 3):
            p = lax.rem(pos[nxt] + k, 4)
            send(
                ("2", u, k), acc2.at[u, pl.ds(pl.multiple_of(p * 64, 64), 64)], in2.at[u, k - 1],
                at(nxt, k), rs, u * 9 + 3 + k - 1,
            )

    def step3(u):
        axis, nxt = (GROUP_OF[u] + 1) % 3, (GROUP_OF[u] + 2) % 3
        for k in (1, 2, 3):
            copies["2", u, k].wait_recv()
        s = acc2[u, pl.ds(pl.multiple_of(pos[axis] * 64, 64), 64), :].astype(F32)
        for k in range(3):
            s = s + in2[u, k].astype(F32)
        acc3[u] = s.astype(BF16)
        for k in (1, 2, 3):
            p = lax.rem(pos[nxt] + k, 4)
            send(
                ("3", u, k), acc3.at[u, pl.ds(pl.multiple_of(p * 16, 16), 16)], in3.at[u, k - 1],
                at(nxt, k), rs, u * 9 + 6 + k - 1,
            )

    def own_rows(g, level):
        p1, p2, p3 = pos[g], pos[(g + 1) % 3], pos[(g + 2) % 3]
        if level == 3:
            return p1, pl.ds(pl.multiple_of(p2 * 64 + p3 * 16, 16), 16)
        if level == 2:
            return p1, pl.ds(pl.multiple_of(p2 * 64, 64), 64)
        return p1, pl.ds(0, 256)

    def step4(u):
        axis = (GROUP_OF[u] + 2) % 3
        for k in (1, 2, 3):
            copies["3", u, k].wait_recv()
        s = acc3[u, pl.ds(pl.multiple_of(pos[axis] * 16, 16), 16), :].astype(F32)
        for k in range(3):
            s = s + in3[u, k].astype(F32)
        p1, rows = own_rows(GROUP_OF[u], 3)
        gath[core, p1, PLACE[u], rows, :] = s.astype(BF16)
        return jnp.sum(s * s)

    def back(l):
        lo, count = 5 - l, 18 + 2 * l
        half = count // 2
        for start in (lo, lo + half):
            rows = slice(start - lo, start - lo + half)
            d = up[start - 2 : start - 2 + half] * fac[l, start : start + half]
            store3(dy3, start, half, d, -1)
        d = dy3[6:22, :, 256:512].astype(F32) * in_tile
        store3(dym, 1, 16, d, -1)

    def weights(l):
        xt[...] = turn(x3[l, 5:23, :, 256:512], 18)
        block = 4 + 9 * (2 - l)
        for a in range(3):
            if a == 1:
                g = nn(xt[...], dym[...].reshape(18 * WIDE, 768))
            else:
                g = nn(xt[:, 64 * a : 64 * a + 1024], dym[1:17].reshape(16 * WIDE, 768))
            g = g.astype(BF16)
            for b in range(3):
                for e in range(2):
                    grad[e, block + 3 * a + b] = g[:, b * 256 + e * 128 : b * 256 + (e + 1) * 128]

    def spread_back(l):
        lo, count = 6 - l, 16 + 2 * l
        half = count // 2
        for start in (lo, lo + half):
            d = jnp.zeros((half * WIDE, 256), F32)
            for a in range(3):
                for b in range(3):
                    src = dy3[start + 1 - a : start + 1 - a + half, :, b * 256 : (b + 1) * 256]
                    d = d + nt(src.reshape(half * WIDE, 256), kern_ref[l, a, b])
            here = slice(start - 2, start - 2 + half)
            up[here] = up[here] + d.reshape(half, WIDE, 256)

    zero_row = jnp.zeros((WIDE, 768), BF16)
    dym[0] = zero_row
    dym[17] = zero_row
    back(2)
    weights(2)
    give_core(0)
    spread_back(2)
    step1(0)
    back(1)
    weights(1)
    give_core(1)
    for u in PIECES[0]:
        step2(u)
    spread_back(1)
    step1(1)
    back(0)
    weights(0)
    for u in PIECES[0]:
        step3(u)
    spread_back(0)
    for u in PIECES[1]:
        step2(u)
    squares = jnp.zeros((), F32)
    dx0 = (up[4:20] * in_tile).astype(BF16).reshape(8, 2, WIDE, 256)
    mt = mean[3:11].reshape(512, 128).T.astype(BF16)
    ge = nn(mt[0:64], dx0[:, 0].reshape(512, 256)) + nn(mt[64:128], dx0[:, 1].reshape(512, 256))
    for e in range(2):
        grad[e, 31] = jnp.zeros((256, 128), BF16)
        grad[e, 31, 0:64, :] = ge[:, e * 128 : (e + 1) * 128].astype(BF16)
    give_core(2)
    for u in PIECES[0]:
        squares = squares + step4(u)
    step1(2)
    for u in PIECES[1]:
        step3(u)
    for u in PIECES[2]:
        step2(u)
    for u in PIECES[1]:
        squares = squares + step4(u)
    for u in PIECES[2]:
        step3(u)
    for u in PIECES[2]:
        squares = squares + step4(u)

    p1, rows = own_rows(2, 3)
    full = jnp.full((8, 128), squares, F32)
    high = full.astype(BF16).astype(F32)
    gath[core, p1, 8, rows, :] = jnp.concatenate([high, full - high], 0).astype(BF16)

    for level in (3, 2, 1):
        for g in range(3):
            axis = (g + level - 1) % 3
            if level < 3:
                for k in (1, 2, 3):
                    copies["g", level + 1, g, k].wait_recv()
            p1, rows = own_rows(g, level)
            part = gath.at[core, p1, pl.ds(3 * g, 3), rows, :]
            for k in (1, 2, 3):
                send(("g", level, g, k), part, part, at(axis, k), ag, g * 9 + (3 - level) * 3 + k - 1)
    for g in range(3):
        part = gath.at[core, pos[g], pl.ds(3 * g, 3)]
        send(("h", g, 0), part, part, other, ag, 27 + g * 4)
    for k in (1, 2, 3):
        for g in range(3):
            copies["g", 1, g, k].wait_recv()
            part = gath.at[core, lax.rem(pos[g] + 4 - k, 4), pl.ds(3 * g, 3)]
            send(("h", g, k), part, part, other, ag, 27 + g * 4 + k)
    for g in range(3):
        for k in range(4):
            copies["h", g, k].wait_recv()

    stats = jnp.zeros((1, 128), F32)
    for e in range(2):
        for p in range(4):
            stats = stats + jnp.sum(gath[e, p, 8].astype(F32), axis=0, keepdims=True)
    entries = 31 * 65536 + 16384
    scale = 1.0 / jnp.sqrt(stats / (8.0 * entries) + 1e-06)
    for u in range(8):
        for p in range(4):
            block = 4 * u + p
            for e in range(2):
                v = (gath[e, p, PLACE[u]].astype(F32) * scale).astype(BF16)
                lanes = slice(e * 128, (e + 1) * 128)
                if block < 4:
                    dup_ref[block, :, lanes] = v
                elif block == 31:
                    eup_ref[:, lanes] = v[0:64]
                else:
                    l, tap = 2 - (block - 4) // 9, (block - 4) % 9
                    kup_ref[9 * l + tap, :, lanes] = v
    for c in cot_copies + mean_copies:
        c.wait_send()
    for c in copies.values():
        c.wait_send()


def on_device(records, cell_ids, counts, embed, kernels, down, cotangent):
    slot = jnp.arange(16, dtype=jnp.int32)[None, None, :]
    ids = jnp.where(slot < counts[:, :, None], cell_ids, -1)
    values = lax.all_to_all(records, ("lat", "lon"), split_axis=1, concat_axis=0, tiled=True).reshape(128, 1024)
    ids = lax.all_to_all(ids, ("lat", "lon"), split_axis=1, concat_axis=0, tiled=True).reshape(128, 16)
    vmem = pl.BlockSpec(memory_space=pltpu.VMEM)
    coarse, kup, dup, eup = pl.pallas_call(
        body,
        out_shape=(
            jax.ShapeDtypeStruct((8, 24, 256), BF16),
            jax.ShapeDtypeStruct((27, 256, 256), BF16),
            jax.ShapeDtypeStruct((4, 256, 256), BF16),
            jax.ShapeDtypeStruct((64, 256), BF16),
        ),
        in_specs=[vmem] * 7,
        out_specs=(vmem,) * 4,
        scratch_shapes=[
            pltpu.VMEM((384, 2048), BF16),
            pltpu.VMEM((2048, 256), BF16),
            pltpu.VMEM((14, WIDE, 128), F32),
            pltpu.VMEM((12, 40, 256), F32),
            pltpu.VMEM((2, 12 * WIDE, 128), F32),
            pltpu.VMEM((2, 12 * WIDE, 128), F32),
            pltpu.VMEM((12, WIDE, 512), BF16),
            pltpu.VMEM((24, WIDE, 256), F32),
            pltpu.VMEM((3, ROWS, WIDE, 768), BF16),
            pltpu.VMEM((3, ROWS, WIDE, 256), F32),
            pltpu.VMEM((ROWS, WIDE, 768), BF16),
            pltpu.VMEM((18, WIDE, 768), BF16),
            pltpu.VMEM((256, 18 * WIDE), BF16),
            pltpu.VMEM((ROWS, WIDE, 256), BF16),
            pltpu.VMEM((2, 512, 128), F32),
                pltpu.VMEM((2, 32, 256, 128), BF16),
            pltpu.VMEM((32, 256, 128), BF16),
            pltpu.VMEM((32, 256, 128), BF16),
            pltpu.VMEM((8, 3, 256, 128), BF16),
            pltpu.VMEM((8, 256, 128), BF16),
            pltpu.VMEM((8, 3, 64, 128), BF16),
            pltpu.VMEM((8, 64, 128), BF16),
            pltpu.VMEM((8, 3, 16, 128), BF16),
            pltpu.VMEM((2, 4, 9, 256, 128), BF16),
            pltpu.SemaphoreType.DMA((2, 8)),
            pltpu.SemaphoreType.DMA((2, 8)),
            pltpu.SemaphoreType.DMA((75,)),
            pltpu.SemaphoreType.DMA((75,)),
            pltpu.SemaphoreType.DMA((39,)),
            pltpu.SemaphoreType.DMA((39,)),
        ],
        compiler_params=pltpu.CompilerParams(
            collective_id=0, has_side_effects=True, vmem_limit_bytes=60 * 1024 * 1024
        ),
    )(values, ids, ids.T, embed, kernels, down, cotangent)
    return coarse, kup.reshape(3, 3, 3, 256, 256), dup.reshape(2, 2, 256, 256), eup


def solution(mesh):
    return jax.shard_map(
        on_device,
        mesh=mesh,
        in_specs=(
            P(("lat", "lon"), None, None),
            P(("lat", "lon"), None, None),
            P(("lat", "lon"), None),
            P(),
            P(),
            P(),
            P("lat", "lon", None),
        ),
        out_specs=(P("lat", "lon", None), P(), P(), P()),
        check_vma=False,
    )
```

```python
import jax
import jax.numpy as jnp
from jax import lax
from jax.experimental import pallas as pl
from jax.experimental.pallas import tpu as pltpu
from jax.sharding import PartitionSpec as P

F32 = jnp.float32
BF16 = jnp.bfloat16
MESH = pl.DeviceIdType.MESH

ROWS, WIDE = 28, 64
PIECES = ((0, 1, 2), (3, 4), (5, 6, 7))
GROUPS = ((0, 3, 6), (1, 4, 7), (2, 5))
GROUP_OF = {u: g for g, us in enumerate(GROUPS) for u in us}
PLACE = {u: g * 3 + i for g, us in enumerate(GROUPS) for i, u in enumerate(us)}


def nn(a, b):
    return jnp.dot(a, b, preferred_element_type=F32)


def nt(a, b):
    return lax.dot_general(a, b, (((1,), (1,)), ((), ())), preferred_element_type=F32)


def body(
    records_ref, ids_ref, counts_ref, embed_ref, kern_hbm, down_hbm, cot_ref,
    coarse_ref, gath, scale_ref,
    kern_ref, down_ref, table, arr1, out2, in2,
    onehot, spread, mean, cpad, fine_e, fine_o, eo, up, x3, fac, dy3, dym, xt, xl, ybuf,
    grad, core_in, acc1, in1, acc2, in2r, acc3, in3,
    load_s, d1_s, d1_r, d2_s, d2_r, halo_s, halo_r, rs_s, rs_r, ag_s, ag_r,
):
    loads = [
        pltpu.make_async_copy(kern_hbm, kern_ref, load_s.at[0]),
        pltpu.make_async_copy(down_hbm, down_ref, load_s.at[1]),
    ]
    for c in loads:
        c.start()
    lat = lax.axis_index("lat")
    lon = lax.axis_index("lon")
    xx = lax.rem(lon // 2, 2) * 2 + lat // 4
    yy = lax.rem(lat, 4)
    zz = lon // 4
    core = lax.rem(lon, 2)
    pos = (xx, yy, zz)

    def at(axis, k):
        c = list(pos)
        c[axis] = lax.rem(c[axis] + k, 4)
        return (lax.rem(c[0], 2) * 4 + c[1], c[2] * 4 + (c[0] // 2) * 2 + core)

    other = (lat, lon + 1 - 2 * core)

    def side(dr, dc):
        return (lax.rem(lat + dr + 8, 8), lax.rem(lon + dc + 16, 16))

    sides = [(r, c) for r in (-1, 0, 1) for c in (-1, 0, 1) if (r, c) != (0, 0)]
    partners = [(lax.rem(lat + k, 8), lon) for k in range(1, 8)]
    partners += [(lat, lax.rem(lon + k, 16)) for k in range(1, 16)]
    partners += [side(r, c) for r in (-1, 1) for c in (-1, 1)]
    flip = lon + 2 - 4 * lax.rem(lon // 2, 2)
    partners += [(lax.rem(lat + 4, 8), flip)]
    barrier = pltpu.get_barrier_semaphore()
    for who in partners:
        pl.semaphore_signal(barrier, inc=1, device_id=who, device_id_type=MESH)

    live = jnp.broadcast_to(counts_ref[...].astype(F32), (128, 128)).T[:, 0:16]
    slot = lax.broadcasted_iota(jnp.int32, (128, 16), 1).astype(F32)
    cell = jnp.where(slot < live, ids_ref[...], 768)
    kk = lax.broadcasted_iota(jnp.int32, (16, 128), 0)
    ll = lax.broadcasted_iota(jnp.int32, (16, 128), 1)
    lane = (kk >> 3) * 16 + (kk & 7)
    digits = nn((cell >> 5).astype(F32).astype(BF16), jnp.where(ll == lane, 1.0, 0.0).astype(BF16))
    digits = digits + nn((cell & 31).astype(F32).astype(BF16), jnp.where(ll == lane + 8, 1.0, 0.0).astype(BF16))
    table[:, :, 0:1024] = records_ref[...].reshape(8, 16, 1024)
    table[:, :, 1024:1152] = digits.astype(BF16).reshape(8, 16, 128)
    cpad[2:10, 8:32, :] = cot_ref[...].astype(F32)
    pl.semaphore_wait(barrier, len(partners))

    def remote(src, dst, send_sem, recv_sem, who):
        c = pltpu.make_async_remote_copy(
            src_ref=src, dst_ref=dst, send_sem=send_sem, recv_sem=recv_sem, device_id=who, device_id_type=MESH
        )
        c.start()
        return c

    lat_copies = []
    for k in range(1, 8):
        p = lax.rem(lat + k, 8)
        lat_copies.append(remote(table.at[p], arr1.at[lat], d1_s.at[k - 1], d1_r.at[k - 1], (p, lon)))
    arr1[lat] = table[lat]
    for c in lat_copies:
        c.wait_recv()
    flat = arr1[...].reshape(128, 1152)
    rho = lax.broadcasted_iota(jnp.int32, (256, 128), 0)
    came = lax.broadcasted_iota(jnp.int32, (256, 128), 1)
    match = came == (rho & 7) * 16 + (rho >> 4)
    halves = [jnp.where(match & (((rho >> 3) & 1) == h), 1.0, 0.0).astype(BF16) for h in range(2)]
    second = pltpu.roll(flat[:, 1024:1152].astype(F32), 112, 1).astype(BF16)
    moved = nn(halves[0], flat[:, 0:512]) + nn(halves[1], flat[:, 512:1024])
    moved_ids = nn(halves[0], flat[:, 1024:1152]) + nn(halves[1], second)
    out2[:, :, 0:512] = moved.astype(BF16).reshape(16, 16, 512)
    out2[:, :, 512:640] = moved_ids.astype(BF16).reshape(16, 16, 128)
    lon_copies = []
    for k in range(1, 16):
        q = lax.rem(lon + k, 16)
        lon_copies.append(remote(out2.at[q], in2.at[lon], d2_s.at[k - 1], d2_r.at[k - 1], (lat, q)))
    in2[lon] = out2[lon]

    def span(step, rows, lead, cols, near):
        if step[0] == 0:
            r_src = r_dst = (lead, rows)
        elif step[0] < 0:
            r_src, r_dst = (lead, lead), (lead + rows, lead)
        else:
            r_src, r_dst = (rows, lead), (0, lead)
        if step[1] == 0:
            c_src = c_dst = (8, cols)
        elif step[1] < 0:
            c_src, c_dst = (8, 8), (8 + cols, 8)
        else:
            c_src, c_dst = (cols, 8), (0, 8)
        return r_src, c_src, r_dst, c_dst

    def halo(ref, rows, lead, cols, which):
        copies = []
        for n, step in enumerate(sides):
            (a, la), (b, lb), (c, lc), (d, ld) = span(step, rows, lead, cols, None)
            copies.append(
                pltpu.make_async_remote_copy(
                    src_ref=ref.at[pl.ds(a, la), pl.ds(b, lb), :],
                    dst_ref=ref.at[pl.ds(c, lc), pl.ds(d, ld), :],
                    send_sem=halo_s.at[which, n],
                    recv_sem=halo_r.at[which, n],
                    device_id=side(*step),
                    device_id_type=MESH,
                )
            )
        for c in copies:
            c.start()
        return copies

    cot_copies = halo(cpad, 8, 2, 24, 0)

    for c in lon_copies:
        c.wait_recv()
    code = in2[:, :, 512:640].reshape(256, 128).astype(F32)
    code = code * 32.0 + pltpu.roll(code, 120, 1)
    odds = (((code.astype(jnp.int32) * 1366) >> 16) & 1).astype(F32)
    idt = code.T[0:8].astype(jnp.int32)
    rowt = (idt * 1366) >> 16
    place = (rowt >> 1) * 48 + (idt - rowt * 48)
    cells = lax.broadcasted_iota(jnp.int32, (384, 256), 0)
    low = lax.broadcasted_iota(jnp.int32, (256, 128), 1) < 64
    for k in range(8):
        onehot[:, k * 256 : (k + 1) * 256] = jnp.where(cells == place[k : k + 1, :], 1.0, 0.0).astype(BF16)
        odd = odds[:, k : k + 1]
        flag = jnp.where(low, 1.0 - odd, odd)
        pair = in2[:, :, (k // 2) * 128 : (k // 2 + 1) * 128].reshape(256, 128).astype(F32)
        swap = pltpu.roll(pair, 64, 1)
        both = jnp.where(low, pair, swap) if k % 2 == 0 else jnp.where(low, swap, pair)
        spread[k * 256 : (k + 1) * 256, 0:128] = (both * flag).astype(BF16)
        spread[k * 256 : (k + 1) * 256, 128:256] = flag.astype(BF16)
    sums = nn(onehot[...], spread[...])
    means = (sums[:, 0:128] / jnp.maximum(sums[:, 128:256], 1.0)).astype(BF16).astype(F32)
    mean[3:11, 8:56, :] = means.reshape(8, 48, 128)
    mean_copies = halo(mean, 8, 3, 48, 1)

    for c in loads:
        c.wait()
    for c in cot_copies:
        c.wait_recv()
    fine_e[...] = jnp.zeros_like(fine_e)
    fine_o[...] = jnp.zeros_like(fine_o)
    coarse_cells = cpad[:, 4:36, :].reshape(384, 256)
    for h in range(2):
        part = coarse_cells[:, h * 128 : (h + 1) * 128]
        fine_e[h, pl.ds(0, 384, stride=2), :] = part
        fine_o[h, pl.ds(1, 384, stride=2), :] = part
    for h in range(2):
        eo[:, :, h * 128 : (h + 1) * 128] = fine_e[h].astype(BF16).reshape(12, WIDE, 128)
        eo[:, :, 256 + h * 128 : 256 + (h + 1) * 128] = fine_o[h].astype(BF16).reshape(12, WIDE, 128)
    for a in range(2):
        flat = eo[...].reshape(12 * WIDE, 512)
        top = nt(flat[:, 0:256], down_ref[a, 0]) + nt(flat[:, 256:512], down_ref[a, 1])
        top = top.reshape(12, WIDE, 256)
        for i in range(12):
            up[2 * i + a] = top[i]

    def inside(first, count):
        row = lax.broadcasted_iota(jnp.int32, (count, 1, 1), 0) + (lat * 16 - 6 + first)
        return jnp.where((row >= 0) & (row < 128), 1.0, 0.0)

    column = lax.broadcasted_iota(jnp.int32, (1, WIDE, 1), 1)
    in_tile = jnp.where((column >= 8) & (column < 56), 1.0, 0.0)

    def store3(ref, first, count, value, order):
        flat = value.reshape(count * WIDE, 256)
        prev = pltpu.roll(flat, 1, 0)
        nxt = pltpu.roll(flat, count * WIDE - 1, 0)
        parts = (prev, flat, nxt) if order > 0 else (nxt, flat, prev)
        for b, part in enumerate(parts):
            ref[first : first + count, :, b * 256 : (b + 1) * 256] = part.astype(BF16).reshape(count, WIDE, 256)

    def turn(ref_slice, count):
        return ref_slice.reshape(count * WIDE, 256).T

    for c in mean_copies:
        c.wait_recv()
    for first in (0, 7):
        lhs = mean[first : first + 7].reshape(7 * WIDE, 128).astype(BF16)
        zero = jnp.zeros((64, 256), BF16)
        for par in range(2):
            both = (embed_ref[...], zero) if par == 0 else (zero, embed_ref[...])
            x0 = nn(lhs, jnp.concatenate(both, 0)).reshape(7, WIDE, 256)
            row = lax.broadcasted_iota(jnp.int32, (7, 1, 1), 0) * 2 + (lat * 16 - 6 + 2 * first + par)
            x0 = x0 * jnp.where((row >= 0) & (row < 128), 1.0, 0.0)
            flat = x0.reshape(7 * WIDE, 256)
            parts = (pltpu.roll(flat, 1, 0), flat, pltpu.roll(flat, 7 * WIDE - 1, 0))
            for b, part in enumerate(parts):
                part = part.astype(BF16).reshape(7, WIDE, 256)
                for i in range(7):
                    x3[0, 2 * (first + i) + par, :, b * 256 : (b + 1) * 256] = part[i]

    for l in range(3):
        first, count = l + 1, 26 - 2 * l
        half = count // 2
        for start in (first, first + half):
            y = jnp.zeros((half * WIDE, 256), F32)
            for a in range(3):
                y = y + nn(
                    x3[l, start + a - 1 : start + a - 1 + half].reshape(half * WIDE, 768),
                    kern_ref[l, a].reshape(768, 256),
                )
            s = jax.nn.sigmoid(y)
            gain = (s * (1.0 + y * (1.0 - s))).reshape(half, WIDE, 256)
            keep = inside(start, half)
            fac[l, start : start + half] = gain * keep
            x = x3[l, start : start + half, :, 256:512].reshape(half * WIDE, 256).astype(F32)
            x = (x + y * s).reshape(half, WIDE, 256)
            if l < 2:
                store3(x3.at[l + 1], start, half, x * keep, 1)
            else:
                xl[start : start + half] = (x * in_tile).astype(BF16)

    sum0 = jnp.zeros((512, 256), F32)
    sum1 = jnp.zeros((512, 256), F32)
    last = xl[6:22].reshape(8, 2, WIDE, 256)
    rights = eo[2:10].reshape(512, 512)
    for a in range(2):
        piece = last[:, a].reshape(512, 256)
        sum0 = sum0 + nn(piece, down_ref[a, 0])
        sum1 = sum1 + nn(piece, down_ref[a, 1])
        g = nn(piece.T, rights).astype(BF16)
        for b in range(2):
            for e in range(2):
                grad[e, 2 * a + b] = g[:, b * 256 + e * 128 : b * 256 + (e + 1) * 128]
    total = sum0 + pltpu.roll(sum1, 511, 0)
    for h in range(2):
        ybuf[h] = total[:, h * 128 : (h + 1) * 128]
    for h in range(2):
        picked = ybuf[h, pl.ds(0, 256, stride=2), :].reshape(8, 32, 128)
        coarse_ref[:, :, h * 128 : (h + 1) * 128] = picked[:, 4:28].astype(BF16)

    copies = {}

    def send(key, src, dst, who, sems, index):
        c = pltpu.make_async_remote_copy(
            src_ref=src, dst_ref=dst, send_sem=sems[0].at[index], recv_sem=sems[1].at[index],
            device_id=who, device_id_type=MESH,
        )
        c.start()
        copies[key] = c

    rs = (rs_s, rs_r)
    ag = (ag_s, ag_r)

    def give_core(piece):
        b0, n = 4 * PIECES[piece][0], 4 * len(PIECES[piece])
        send(
            ("c", piece), grad.at[1 - core, pl.ds(b0, n)], core_in.at[pl.ds(b0, n)], other, rs, 72 + piece
        )

    def step1(piece):
        copies["c", piece].wait_recv()
        for u in PIECES[piece]:
            for p in range(4):
                acc1[4 * u + p] = (grad[core, 4 * u + p].astype(F32) + core_in[4 * u + p].astype(F32)).astype(BF16)
            axis = GROUP_OF[u]
            for k in (1, 2, 3):
                p = lax.rem(pos[axis] + k, 4)
                send(("1", u, k), acc1.at[4 * u + p], in1.at[u, k - 1], at(axis, k), rs, u * 9 + k - 1)

    def step2(u):
        axis, nxt = GROUP_OF[u], (GROUP_OF[u] + 1) % 3
        for k in (1, 2, 3):
            copies["1", u, k].wait_recv()
        s = acc1[4 * u + pos[axis]].astype(F32)
        for k in range(3):
            s = s + in1[u, k].astype(F32)
        acc2[u] = s.astype(BF16)
        for k in (1, 2, 3):
            p = lax.rem(pos[nxt] + k, 4)
            send(
                ("2", u, k), acc2.at[u, pl.ds(pl.multiple_of(p * 64, 64), 64)], in2r.at[u, k - 1],
                at(nxt, k), rs, u * 9 + 3 + k - 1,
            )

    def step3(u):
        axis, nxt = (GROUP_OF[u] + 1) % 3, (GROUP_OF[u] + 2) % 3
        for k in (1, 2, 3):
            copies["2", u, k].wait_recv()
        s = acc2[u, pl.ds(pl.multiple_of(pos[axis] * 64, 64), 64), :].astype(F32)
        for k in range(3):
            s = s + in2r[u, k].astype(F32)
        acc3[u] = s.astype(BF16)
        for k in (1, 2, 3):
            p = lax.rem(pos[nxt] + k, 4)
            send(
                ("3", u, k), acc3.at[u, pl.ds(pl.multiple_of(p * 16, 16), 16)], in3.at[u, k - 1],
                at(nxt, k), rs, u * 9 + 6 + k - 1,
            )

    def own_rows(g, level):
        p1, p2, p3 = pos[g], pos[(g + 1) % 3], pos[(g + 2) % 3]
        if level == 3:
            return p1, pl.ds(pl.multiple_of(p2 * 64 + p3 * 16, 16), 16)
        if level == 2:
            return p1, pl.ds(pl.multiple_of(p2 * 64, 64), 64)
        return p1, pl.ds(0, 256)

    def step4(u):
        axis = (GROUP_OF[u] + 2) % 3
        for k in (1, 2, 3):
            copies["3", u, k].wait_recv()
        s = acc3[u, pl.ds(pl.multiple_of(pos[axis] * 16, 16), 16), :].astype(F32)
        for k in range(3):
            s = s + in3[u, k].astype(F32)
        p1, rows = own_rows(GROUP_OF[u], 3)
        gath[core, p1, PLACE[u], rows, :] = s.astype(BF16)
        return jnp.sum(s * s)

    def back(l):
        lo, count = 5 - l, 18 + 2 * l
        half = count // 2
        for start in (lo, lo + half):
            rows = slice(start - lo, start - lo + half)
            d = up[start - 2 : start - 2 + half] * fac[l, start : start + half]
            store3(dy3, start, half, d, -1)
        d = dy3[6:22, :, 256:512].astype(F32) * in_tile
        store3(dym, 1, 16, d, -1)

    def weights(l):
        xt[...] = turn(x3[l, 5:23, :, 256:512], 18)
        block = 4 + 9 * (2 - l)
        for a in range(3):
            if a == 1:
                g = nn(xt[...], dym[...].reshape(18 * WIDE, 768))
            else:
                g = nn(xt[:, 64 * a : 64 * a + 1024], dym[1:17].reshape(16 * WIDE, 768))
            g = g.astype(BF16)
            for b in range(3):
                for e in range(2):
                    grad[e, block + 3 * a + b] = g[:, b * 256 + e * 128 : b * 256 + (e + 1) * 128]

    def spread_back(l):
        lo, count = 6 - l, 16 + 2 * l
        half = count // 2
        for start in (lo, lo + half):
            d = jnp.zeros((half * WIDE, 256), F32)
            for a in range(3):
                for b in range(3):
                    src = dy3[start + 1 - a : start + 1 - a + half, :, b * 256 : (b + 1) * 256]
                    d = d + nt(src.reshape(half * WIDE, 256), kern_ref[l, a, b])
            here = slice(start - 2, start - 2 + half)
            up[here] = up[here] + d.reshape(half, WIDE, 256)

    zero_row = jnp.zeros((WIDE, 768), BF16)
    dym[0] = zero_row
    dym[17] = zero_row
    back(2)
    weights(2)
    give_core(0)
    spread_back(2)
    step1(0)
    back(1)
    weights(1)
    give_core(1)
    for u in PIECES[0]:
        step2(u)
    spread_back(1)
    step1(1)
    back(0)
    weights(0)
    for u in PIECES[0]:
        step3(u)
    spread_back(0)
    for u in PIECES[1]:
        step2(u)
    squares = jnp.zeros((), F32)
    dx0 = (up[4:20] * in_tile).astype(BF16).reshape(8, 2, WIDE, 256)
    mt = mean[3:11].reshape(512, 128).T.astype(BF16)
    ge = nn(mt[0:64], dx0[:, 0].reshape(512, 256)) + nn(mt[64:128], dx0[:, 1].reshape(512, 256))
    for e in range(2):
        grad[e, 31] = jnp.zeros((256, 128), BF16)
        grad[e, 31, 0:64, :] = ge[:, e * 128 : (e + 1) * 128].astype(BF16)
    give_core(2)
    for u in PIECES[0]:
        squares = squares + step4(u)
    step1(2)
    for u in PIECES[1]:
        step3(u)
    for u in PIECES[2]:
        step2(u)
    for u in PIECES[1]:
        squares = squares + step4(u)
    for u in PIECES[2]:
        step3(u)
    for u in PIECES[2]:
        squares = squares + step4(u)

    p1, rows = own_rows(2, 3)
    full = jnp.full((8, 128), squares, F32)
    high = full.astype(BF16).astype(F32)
    gath[core, p1, 8, rows, :] = jnp.concatenate([high, full - high], 0).astype(BF16)

    for level in (3, 2, 1):
        for g in range(3):
            axis = (g + level - 1) % 3
            if level < 3:
                for k in (1, 2, 3):
                    copies["g", level + 1, g, k].wait_recv()
            p1, rows = own_rows(g, level)
            part = gath.at[core, p1, pl.ds(3 * g, 3), rows, :]
            for k in (1, 2, 3):
                send(("g", level, g, k), part, part, at(axis, k), ag, g * 9 + (3 - level) * 3 + k - 1)
    for g in range(3):
        part = gath.at[core, pos[g], pl.ds(3 * g, 3)]
        send(("h", g, 0), part, part, other, ag, 27 + g * 4)
    for k in (1, 2, 3):
        for g in range(3):
            copies["g", 1, g, k].wait_recv()
            part = gath.at[core, lax.rem(pos[g] + 4 - k, 4), pl.ds(3 * g, 3)]
            send(("h", g, k), part, part, other, ag, 27 + g * 4 + k)
    for g in range(3):
        for k in range(4):
            copies["h", g, k].wait_recv()

    stats = jnp.zeros((1, 128), F32)
    for e in range(2):
        for p in range(4):
            stats = stats + jnp.sum(gath[e, p, 8].astype(F32), axis=0, keepdims=True)
    entries = 31 * 65536 + 16384
    scale_ref[...] = jnp.broadcast_to(1.0 / jnp.sqrt(stats / (8.0 * entries) + 1e-06), (8, 128))
    for c in lat_copies + lon_copies + cot_copies + mean_copies:
        c.wait_send()
    for c in copies.values():
        c.wait_send()


def finish(gath_hbm, coarse_hbm, scale_ref, coarse_out, kup_out, dup_out, eup_out, gin, kup, dup, eup, in_s, out_s):
    through = pltpu.make_async_copy(coarse_hbm, coarse_out, out_s.at[0])
    through.start()
    reads = []
    for u in range(8):
        c = pltpu.make_async_copy(gath_hbm.at[:, :, PLACE[u]], gin.at[u], in_s.at[u])
        c.start()
        reads.append(c)
    scale = scale_ref[0:1, :]
    writes = [through]

    def write(src, dst, index):
        c = pltpu.make_async_copy(src, dst, out_s.at[index])
        c.start()
        writes.append(c)

    for u in range(8):
        reads[u].wait()
        for p in range(4):
            block = 4 * u + p
            for e in range(2):
                lanes = slice(e * 128, (e + 1) * 128)
                if block == 31:
                    eup[:, lanes] = (gin[u, e, p, 0:64].astype(F32) * scale).astype(BF16)
                    continue
                v = (gin[u, e, p].astype(F32) * scale).astype(BF16)
                if block < 4:
                    dup[block, :, lanes] = v
                else:
                    kup[9 * (2 - (block - 4) // 9) + (block - 4) % 9, :, lanes] = v
            if block == 3:
                write(dup, dup_out, 1)
            elif block == 31:
                write(eup, eup_out, 2)
            elif (block - 4) % 9 == 8:
                l = 2 - (block - 4) // 9
                write(kup.at[pl.ds(9 * l, 9)], kup_out.at[pl.ds(9 * l, 9)], 3 + l)
    for c in writes:
        c.wait()


def on_device(records, cell_ids, counts, embed, kernels, down, cotangent):
    vmem = pl.BlockSpec(memory_space=pltpu.VMEM)
    hbm = pl.BlockSpec(memory_space=pl.ANY)
    coarse, gath, scale = pl.pallas_call(
        body,
        out_shape=(
            jax.ShapeDtypeStruct((8, 24, 256), BF16),
            jax.ShapeDtypeStruct((2, 4, 9, 256, 128), BF16),
            jax.ShapeDtypeStruct((8, 128), F32),
        ),
        in_specs=[vmem, vmem, vmem, vmem, hbm, hbm, vmem],
        out_specs=(vmem,) * 3,
        scratch_shapes=[
            pltpu.VMEM((3, 3, 3, 256, 256), BF16),
            pltpu.VMEM((2, 2, 256, 256), BF16),
            pltpu.VMEM((8, 16, 1152), BF16),
            pltpu.VMEM((8, 16, 1152), BF16),
            pltpu.VMEM((16, 16, 640), BF16),
            pltpu.VMEM((16, 16, 640), BF16),
            pltpu.VMEM((384, 2048), BF16),
            pltpu.VMEM((2048, 256), BF16),
            pltpu.VMEM((14, WIDE, 128), F32),
            pltpu.VMEM((12, 40, 256), F32),
            pltpu.VMEM((2, 12 * WIDE, 128), F32),
            pltpu.VMEM((2, 12 * WIDE, 128), F32),
            pltpu.VMEM((12, WIDE, 512), BF16),
            pltpu.VMEM((24, WIDE, 256), F32),
            pltpu.VMEM((3, ROWS, WIDE, 768), BF16),
            pltpu.VMEM((3, ROWS, WIDE, 256), F32),
            pltpu.VMEM((ROWS, WIDE, 768), BF16),
            pltpu.VMEM((18, WIDE, 768), BF16),
            pltpu.VMEM((256, 18 * WIDE), BF16),
            pltpu.VMEM((ROWS, WIDE, 256), BF16),
            pltpu.VMEM((2, 512, 128), F32),
                pltpu.VMEM((2, 32, 256, 128), BF16),
            pltpu.VMEM((32, 256, 128), BF16),
            pltpu.VMEM((32, 256, 128), BF16),
            pltpu.VMEM((8, 3, 256, 128), BF16),
            pltpu.VMEM((8, 256, 128), BF16),
            pltpu.VMEM((8, 3, 64, 128), BF16),
            pltpu.VMEM((8, 64, 128), BF16),
            pltpu.VMEM((8, 3, 16, 128), BF16),
            pltpu.SemaphoreType.DMA((2,)),
            pltpu.SemaphoreType.DMA((7,)),
            pltpu.SemaphoreType.DMA((7,)),
            pltpu.SemaphoreType.DMA((15,)),
            pltpu.SemaphoreType.DMA((15,)),
            pltpu.SemaphoreType.DMA((2, 8)),
            pltpu.SemaphoreType.DMA((2, 8)),
            pltpu.SemaphoreType.DMA((75,)),
            pltpu.SemaphoreType.DMA((75,)),
            pltpu.SemaphoreType.DMA((39,)),
            pltpu.SemaphoreType.DMA((39,)),
        ],
        compiler_params=pltpu.CompilerParams(
            collective_id=0, has_side_effects=True, vmem_limit_bytes=60 * 1024 * 1024
        ),
    )(records.reshape(128, 1024), cell_ids.reshape(128, 16), counts, embed, kernels, down, cotangent)
    coarse, kup, dup, eup = pl.pallas_call(
        finish,
        out_shape=(
            jax.ShapeDtypeStruct((8, 24, 256), BF16),
            jax.ShapeDtypeStruct((27, 256, 256), BF16),
            jax.ShapeDtypeStruct((4, 256, 256), BF16),
            jax.ShapeDtypeStruct((64, 256), BF16),
        ),
        in_specs=[hbm, hbm, vmem],
        out_specs=(hbm,) * 4,
        scratch_shapes=[
            pltpu.VMEM((8, 2, 4, 256, 128), BF16),
            pltpu.VMEM((27, 256, 256), BF16),
            pltpu.VMEM((4, 256, 256), BF16),
            pltpu.VMEM((64, 256), BF16),
            pltpu.SemaphoreType.DMA((8,)),
            pltpu.SemaphoreType.DMA((6,)),
        ],
        compiler_params=pltpu.CompilerParams(vmem_limit_bytes=24 * 1024 * 1024),
    )(gath, coarse, scale)
    return coarse, kup.reshape(3, 3, 3, 256, 256), dup.reshape(2, 2, 256, 256), eup


def solution(mesh):
    return jax.shard_map(
        on_device,
        mesh=mesh,
        in_specs=(
            P(("lat", "lon"), None, None),
            P(("lat", "lon"), None, None),
            P(("lat", "lon"), None),
            P(),
            P(),
            P(),
            P("lat", "lon", None),
        ),
        out_specs=(P("lat", "lon", None), P(), P(), P()),
        check_vma=False,
    )
```

```python
import jax
import jax.numpy as jnp
from jax import lax
from jax.experimental import pallas as pl
from jax.experimental.pallas import tpu as pltpu
from jax.sharding import PartitionSpec as P

F32 = jnp.float32
BF16 = jnp.bfloat16
MESH = pl.DeviceIdType.MESH

ROWS, WIDE = 28, 64
PIECES = ((0,), (1, 2), (3, 4), (5, 6), (7,))
PLANE = [(kb, kc) for kb in range(4) for kc in range(4) if (kb, kc) != (0, 0)]


def nn(a, b):
    return jnp.dot(a, b, preferred_element_type=F32)


def nt(a, b):
    return lax.dot_general(a, b, (((1,), (1,)), ((), ())), preferred_element_type=F32)


def body(
    records_ref, ids_ref, counts_ref, embed_ref, kern_hbm, down_hbm, cot_ref,
    coarse_ref, gath_hbm, scale_ref,
    kern_ref, down_ref, table, arr1, out2, in2,
    onehot, spread, mean, cpad, fine_e, fine_o, eo, up, x3, fac, dy3, dym, xt, xl, ybuf,
    grad, core_in, acc1, in1, acc2, in2r, gath,
    load_s, d1_s, d1_r, d2_s, d2_r, halo_s, halo_r, sum_s, sum_r, out_s,
):
    loads = [
        pltpu.make_async_copy(kern_hbm, kern_ref, load_s.at[0]),
        pltpu.make_async_copy(down_hbm, down_ref, load_s.at[1]),
    ]
    for c in loads:
        c.start()
    lat = lax.axis_index("lat")
    lon = lax.axis_index("lon")
    xx = lax.rem(lon // 2, 2) * 2 + lat // 4
    yy = lax.rem(lat, 4)
    zz = lon // 4
    core = lax.rem(lon, 2)
    pos = (xx, yy, zz)

    def by(offsets):
        c = [lax.rem(p + o, 4) for p, o in zip(pos, offsets)]
        return (lax.rem(c[0], 2) * 4 + c[1], c[2] * 4 + (c[0] // 2) * 2 + core)

    def along(axis, k):
        return by([k if i == axis else 0 for i in range(3)])

    def across(axis, kb, kc):
        b, c = (axis + 1) % 3, (axis + 2) % 3
        return by([kb if i == b else kc if i == c else 0 for i in range(3)])

    other = (lat, lon + 1 - 2 * core)

    def side(dr, dc):
        return (lax.rem(lat + dr + 8, 8), lax.rem(lon + dc + 16, 16))

    sides = [(r, c) for r in (-1, 0, 1) for c in (-1, 0, 1) if (r, c) != (0, 0)]
    partners = [by((dx, dy, 0)) for dx, dy in PLANE]
    partners += [by((0, dy, dz)) for dy in range(4) for dz in (1, 2, 3)]
    partners += [by((dx, 0, dz)) for dx in (1, 2, 3) for dz in (1, 2, 3)]
    partners += [(lat, lax.rem(lon + k, 16)) for k in range(1, 16, 2)]
    partners += [side(r, c) for r in (-1, 1) for c in (-1, 1)]
    barrier = pltpu.get_barrier_semaphore()
    for who in partners:
        pl.semaphore_signal(barrier, inc=1, device_id=who, device_id_type=MESH)

    cell = jnp.where(lax.broadcasted_iota(jnp.int32, (16, 128), 0) < counts_ref[...], ids_ref[...], 768)
    kk = lax.broadcasted_iota(jnp.int32, (128, 16), 1)
    ll = lax.broadcasted_iota(jnp.int32, (128, 16), 0)
    lane = (kk >> 3) * 16 + (kk & 7)
    digits = nn(jnp.where(ll == lane, 1.0, 0.0).astype(BF16), (cell >> 5).astype(F32).astype(BF16))
    digits = digits + nn(jnp.where(ll == lane + 8, 1.0, 0.0).astype(BF16), (cell & 31).astype(F32).astype(BF16))
    digits = digits.T
    table[:, :, 0:1024] = records_ref[...].reshape(8, 16, 1024)
    table[:, :, 1024:1152] = digits.astype(BF16).reshape(8, 16, 128)
    cpad[2:10, 8:32, :] = cot_ref[...].astype(F32)
    pl.semaphore_wait(barrier, len(partners))

    def remote(src, dst, send_sem, recv_sem, who):
        c = pltpu.make_async_remote_copy(
            src_ref=src, dst_ref=dst, send_sem=send_sem, recv_sem=recv_sem, device_id=who, device_id_type=MESH
        )
        c.start()
        return c

    lat_copies = []
    for k in range(1, 8):
        p = lax.rem(lat + k, 8)
        lat_copies.append(remote(table.at[p], arr1.at[lat], d1_s.at[k - 1], d1_r.at[k - 1], (p, lon)))
    arr1[lat] = table[lat]
    for c in lat_copies:
        c.wait_recv()
    flat = arr1[...].reshape(128, 1152)
    rho = lax.broadcasted_iota(jnp.int32, (256, 128), 0)
    came = lax.broadcasted_iota(jnp.int32, (256, 128), 1)
    match = came == (rho & 7) * 16 + (rho >> 4)
    halves = [jnp.where(match & (((rho >> 3) & 1) == h), 1.0, 0.0).astype(BF16) for h in range(2)]
    second = pltpu.roll(flat[:, 1024:1152].astype(F32), 112, 1).astype(BF16)
    moved = nn(halves[0], flat[:, 0:512]) + nn(halves[1], flat[:, 512:1024])
    moved_ids = nn(halves[0], flat[:, 1024:1152]) + nn(halves[1], second)
    out2[:, :, 0:512] = moved.astype(BF16).reshape(16, 16, 512)
    out2[:, :, 512:640] = moved_ids.astype(BF16).reshape(16, 16, 128)
    lon_copies = []
    for k in range(1, 16):
        q = lax.rem(lon + k, 16)
        lon_copies.append(remote(out2.at[q], in2.at[lon], d2_s.at[k - 1], d2_r.at[k - 1], (lat, q)))
    in2[lon] = out2[lon]

    def span(step, rows, lead, cols, near):
        if step[0] == 0:
            r_src = r_dst = (lead, rows)
        elif step[0] < 0:
            r_src, r_dst = (lead, lead), (lead + rows, lead)
        else:
            r_src, r_dst = (rows, lead), (0, lead)
        if step[1] == 0:
            c_src = c_dst = (8, cols)
        elif step[1] < 0:
            c_src, c_dst = (8, 8), (8 + cols, 8)
        else:
            c_src, c_dst = (cols, 8), (0, 8)
        return r_src, c_src, r_dst, c_dst

    def halo(ref, rows, lead, cols, which):
        copies = []
        for n, step in enumerate(sides):
            (a, la), (b, lb), (c, lc), (d, ld) = span(step, rows, lead, cols, None)
            copies.append(
                pltpu.make_async_remote_copy(
                    src_ref=ref.at[pl.ds(a, la), pl.ds(b, lb), :],
                    dst_ref=ref.at[pl.ds(c, lc), pl.ds(d, ld), :],
                    send_sem=halo_s.at[which, n],
                    recv_sem=halo_r.at[which, n],
                    device_id=side(*step),
                    device_id_type=MESH,
                )
            )
        for c in copies:
            c.start()
        return copies

    cot_copies = halo(cpad, 8, 2, 24, 0)

    for c in lon_copies:
        c.wait_recv()
    code = in2[:, :, 512:640].reshape(256, 128).astype(F32)
    code = code * 32.0 + pltpu.roll(code, 120, 1)
    odds = (((code.astype(jnp.int32) * 1366) >> 16) & 1).astype(F32)
    idt = code.T[0:8].astype(jnp.int32)
    rowt = (idt * 1366) >> 16
    place = (rowt >> 1) * 48 + (idt - rowt * 48)
    cells = lax.broadcasted_iota(jnp.int32, (384, 256), 0)
    low = lax.broadcasted_iota(jnp.int32, (256, 128), 1) < 64
    for k in range(8):
        onehot[:, k * 256 : (k + 1) * 256] = jnp.where(cells == place[k : k + 1, :], 1.0, 0.0).astype(BF16)
        odd = odds[:, k : k + 1]
        flag = jnp.where(low, 1.0 - odd, odd)
        pair = in2[:, :, (k // 2) * 128 : (k // 2 + 1) * 128].reshape(256, 128).astype(F32)
        swap = pltpu.roll(pair, 64, 1)
        both = jnp.where(low, pair, swap) if k % 2 == 0 else jnp.where(low, swap, pair)
        spread[k * 256 : (k + 1) * 256, 0:128] = (both * flag).astype(BF16)
        spread[k * 256 : (k + 1) * 256, 128:256] = flag.astype(BF16)
    sums = nn(onehot[...], spread[...])
    means = (sums[:, 0:128] / jnp.maximum(sums[:, 128:256], 1.0)).astype(BF16).astype(F32)
    mean[3:11, 8:56, :] = means.reshape(8, 48, 128)
    mean_copies = halo(mean, 8, 3, 48, 1)

    for c in loads:
        c.wait()
    for c in cot_copies:
        c.wait_recv()
    fine_e[...] = jnp.zeros_like(fine_e)
    fine_o[...] = jnp.zeros_like(fine_o)
    coarse_cells = cpad[:, 4:36, :].reshape(384, 256)
    for h in range(2):
        part = coarse_cells[:, h * 128 : (h + 1) * 128]
        fine_e[h, pl.ds(0, 384, stride=2), :] = part
        fine_o[h, pl.ds(1, 384, stride=2), :] = part
    for h in range(2):
        eo[:, :, h * 128 : (h + 1) * 128] = fine_e[h].astype(BF16).reshape(12, WIDE, 128)
        eo[:, :, 256 + h * 128 : 256 + (h + 1) * 128] = fine_o[h].astype(BF16).reshape(12, WIDE, 128)
    for a in range(2):
        flat = eo[...].reshape(12 * WIDE, 512)
        top = nt(flat[:, 0:256], down_ref[a, 0]) + nt(flat[:, 256:512], down_ref[a, 1])
        top = top.reshape(12, WIDE, 256)
        for i in range(12):
            up[2 * i + a] = top[i]

    def inside(first, count):
        row = lax.broadcasted_iota(jnp.int32, (count, 1, 1), 0) + (lat * 16 - 6 + first)
        return jnp.where((row >= 0) & (row < 128), 1.0, 0.0)

    column = lax.broadcasted_iota(jnp.int32, (1, WIDE, 1), 1)
    in_tile = jnp.where((column >= 8) & (column < 56), 1.0, 0.0)

    def store3(ref, first, count, value, order):
        flat = value.reshape(count * WIDE, 256)
        prev = pltpu.roll(flat, 1, 0)
        nxt = pltpu.roll(flat, count * WIDE - 1, 0)
        parts = (prev, flat, nxt) if order > 0 else (nxt, flat, prev)
        for b, part in enumerate(parts):
            ref[first : first + count, :, b * 256 : (b + 1) * 256] = part.astype(BF16).reshape(count, WIDE, 256)

    def turn(ref_slice, count):
        return ref_slice.reshape(count * WIDE, 256).T

    for c in mean_copies:
        c.wait_recv()
    for first in (0, 7):
        lhs = mean[first : first + 7].reshape(7 * WIDE, 128).astype(BF16)
        zero = jnp.zeros((64, 256), BF16)
        for par in range(2):
            both = (embed_ref[...], zero) if par == 0 else (zero, embed_ref[...])
            x0 = nn(lhs, jnp.concatenate(both, 0)).reshape(7, WIDE, 256)
            row = lax.broadcasted_iota(jnp.int32, (7, 1, 1), 0) * 2 + (lat * 16 - 6 + 2 * first + par)
            x0 = x0 * jnp.where((row >= 0) & (row < 128), 1.0, 0.0)
            flat = x0.reshape(7 * WIDE, 256)
            parts = (pltpu.roll(flat, 1, 0), flat, pltpu.roll(flat, 7 * WIDE - 1, 0))
            for b, part in enumerate(parts):
                part = part.astype(BF16).reshape(7, WIDE, 256)
                for i in range(7):
                    x3[0, 2 * (first + i) + par, :, b * 256 : (b + 1) * 256] = part[i]

    for l in range(3):
        first, count = l + 1, 26 - 2 * l
        half = count // 2
        for start in (first, first + half):
            y = jnp.zeros((half * WIDE, 256), F32)
            for a in range(3):
                y = y + nn(
                    x3[l, start + a - 1 : start + a - 1 + half].reshape(half * WIDE, 768),
                    kern_ref[l, a].reshape(768, 256),
                )
            s = jax.nn.sigmoid(y)
            gain = (s * (1.0 + y * (1.0 - s))).reshape(half, WIDE, 256)
            keep = inside(start, half)
            fac[l, start : start + half] = gain * keep
            x = x3[l, start : start + half, :, 256:512].reshape(half * WIDE, 256).astype(F32)
            x = (x + y * s).reshape(half, WIDE, 256)
            if l < 2:
                store3(x3.at[l + 1], start, half, x * keep, 1)
            else:
                xl[start : start + half] = (x * in_tile).astype(BF16)

    sum0 = jnp.zeros((512, 256), F32)
    sum1 = jnp.zeros((512, 256), F32)
    last = xl[6:22].reshape(8, 2, WIDE, 256)
    rights = eo[2:10].reshape(512, 512)
    for a in range(2):
        piece = last[:, a].reshape(512, 256)
        sum0 = sum0 + nn(piece, down_ref[a, 0])
        sum1 = sum1 + nn(piece, down_ref[a, 1])
        g = nn(piece.T, rights).astype(BF16)
        for b in range(2):
            for e in range(2):
                grad[e, 2 * a + b] = g[:, b * 256 + e * 128 : b * 256 + (e + 1) * 128]
    total = sum0 + pltpu.roll(sum1, 511, 0)
    for h in range(2):
        ybuf[h] = total[:, h * 128 : (h + 1) * 128]
    for h in range(2):
        picked = ybuf[h, pl.ds(0, 256, stride=2), :].reshape(8, 32, 128)
        coarse_ref[:, :, h * 128 : (h + 1) * 128] = picked[:, 4:28].astype(BF16)

    copies = {}
    stores = []

    def send(key, src, dst, who, index):
        copies[key] = remote(src, dst, sum_s.at[index], sum_r.at[index], who)

    def rs_core(piece):
        b0, n = 4 * PIECES[piece][0], 4 * len(PIECES[piece])
        send(("c", piece), grad.at[1 - core, pl.ds(b0, n)], core_in.at[pl.ds(b0, n)], other, 37 * 8 + piece)

    def rs_axis(piece):
        copies["c", piece].wait_recv()
        for u in PIECES[piece]:
            for p in range(4):
                acc1[4 * u + p] = (grad[core, 4 * u + p].astype(F32) + core_in[4 * u + p].astype(F32)).astype(BF16)
            for k in (1, 2, 3):
                p = lax.rem(pos[u % 3] + k, 4)
                send(("a", u, k), acc1.at[4 * u + p], in1.at[u, k - 1], along(u % 3, k), u * 37 + k - 1)

    def rs_plane(u):
        axis = u % 3
        for k in (1, 2, 3):
            copies["a", u, k].wait_recv()
        s = acc1[4 * u + pos[axis]].astype(F32)
        for k in range(3):
            s = s + in1[u, k].astype(F32)
        acc2[u] = s.astype(BF16)
        for i, (kb, kc) in enumerate(PLANE):
            row = lax.rem(pos[(axis + 1) % 3] + kb, 4) * 64 + lax.rem(pos[(axis + 2) % 3] + kc, 4) * 16
            src = acc2.at[u, pl.ds(pl.multiple_of(row, 16), 16)]
            send(("b", u, i), src, in2r.at[u, i], across(axis, kb, kc), u * 37 + 3 + i)

    def ag_plane(u):
        axis = u % 3
        for i in range(15):
            copies["b", u, i].wait_recv()
        rows = pl.ds(pl.multiple_of(pos[(axis + 1) % 3] * 64 + pos[(axis + 2) % 3] * 16, 16), 16)
        s = acc2[u, rows, :].astype(F32)
        for i in range(15):
            s = s + in2r[u, i].astype(F32)
        part = gath.at[u, core, pos[axis], rows, :]
        gath[u, core, pos[axis], rows, :] = s.astype(BF16)
        for i, (kb, kc) in enumerate(PLANE):
            send(("p", u, i), part, part, across(axis, kb, kc), u * 37 + 18 + i)

    def ag_axis(u):
        axis = u % 3
        for i in range(15):
            copies["p", u, i].wait_recv()
        part = gath.at[u, core, pos[axis]]
        for k in (1, 2, 3):
            send(("g", u, k), part, part, along(axis, k), u * 37 + 33 + k - 1)

    def ag_core(u):
        for k in (1, 2, 3):
            copies["g", u, k].wait_recv()
        part = gath.at[u, core]
        send(("h", u), part, part, other, u * 37 + 36)

    def square(u):
        copies["h", u].wait_recv()
        c = pltpu.make_async_copy(gath.at[u], gath_hbm.at[u], out_s.at[u])
        c.start()
        stores.append(c)
        total = jnp.zeros((8, 128), F32)
        for e in range(2):
            for p in range(4):
                v = gath[u, e, p].astype(F32)
                total = total + jnp.sum((v * v).reshape(32, 8, 128), axis=0)
        return total

    def back(l):
        lo, count = 5 - l, 18 + 2 * l
        half = count // 2
        for start in (lo, lo + half):
            rows = slice(start - lo, start - lo + half)
            d = up[start - 2 : start - 2 + half] * fac[l, start : start + half]
            store3(dy3, start, half, d, -1)
        d = dy3[6:22, :, 256:512].astype(F32) * in_tile
        store3(dym, 1, 16, d, -1)

    def weights(l):
        xt[...] = turn(x3[l, 5:23, :, 256:512], 18)
        block = 4 + 9 * (2 - l)
        for a in range(3):
            if a == 1:
                g = nn(xt[...], dym[...].reshape(18 * WIDE, 768))
            else:
                g = nn(xt[:, 64 * a : 64 * a + 1024], dym[1:17].reshape(16 * WIDE, 768))
            g = g.astype(BF16)
            for b in range(3):
                for e in range(2):
                    grad[e, block + 3 * a + b] = g[:, b * 256 + e * 128 : b * 256 + (e + 1) * 128]

    def spread_back(l):
        lo, count = 6 - l, 16 + 2 * l
        half = count // 2
        for start in (lo, lo + half):
            d = jnp.zeros((half * WIDE, 256), F32)
            for a in range(3):
                for b in range(3):
                    src = dy3[start + 1 - a : start + 1 - a + half, :, b * 256 : (b + 1) * 256]
                    d = d + nt(src.reshape(half * WIDE, 256), kern_ref[l, a, b])
            here = slice(start - 2, start - 2 + half)
            up[here] = up[here] + d.reshape(half, WIDE, 256)

    zero_row = jnp.zeros((WIDE, 768), BF16)
    dym[0] = zero_row
    dym[17] = zero_row
    def each(step, piece):
        for u in PIECES[piece]:
            step(u)

    def sent(kinds):
        for key in [key for key in copies if key[0] in kinds]:
            copies.pop(key).wait_send()

    rs_core(0)
    back(2)
    rs_axis(0)
    weights(2)
    rs_core(1)
    spread_back(2)
    rs_axis(1)
    back(1)
    weights(1)
    rs_core(2)
    each(rs_plane, 0)
    spread_back(1)
    rs_axis(2)
    back(0)
    weights(0)
    rs_core(3)
    each(rs_plane, 1)
    spread_back(0)
    rs_axis(3)
    dx0 = (up[4:20] * in_tile).astype(BF16).reshape(8, 2, WIDE, 256)
    mt = mean[3:11].reshape(512, 128).T.astype(BF16)
    ge = nn(mt[0:64], dx0[:, 0].reshape(512, 256)) + nn(mt[64:128], dx0[:, 1].reshape(512, 256))
    for e in range(2):
        grad[e, 31] = jnp.zeros((256, 128), BF16)
        grad[e, 31, 0:64, :] = ge[:, e * 128 : (e + 1) * 128].astype(BF16)
    rs_core(4)
    each(ag_plane, 0)
    rs_axis(4)
    each(rs_plane, 2)
    each(ag_plane, 1)
    each(rs_plane, 3)
    each(ag_axis, 0)
    each(rs_plane, 4)
    each(ag_plane, 2)
    each(ag_axis, 1)
    each(ag_plane, 3)
    each(ag_plane, 4)
    each(ag_axis, 2)
    each(ag_core, 0)
    each(ag_axis, 3)
    each(ag_axis, 4)
    squares = square(0)
    each(ag_core, 1)
    for c in lat_copies + lon_copies + cot_copies + mean_copies:
        c.wait_send()
    sent("cab")
    squares = squares + square(1) + square(2)
    each(ag_core, 2)
    sent("p")
    squares = squares + square(3) + square(4)
    each(ag_core, 3)
    squares = squares + square(5) + square(6)
    each(ag_core, 4)
    sent("g")
    squares = squares + square(7)
    entries = 31 * 65536 + 16384
    squares = jnp.sum(jnp.sum(squares, axis=0, keepdims=True), axis=1, keepdims=True)
    scale_ref[...] = jnp.broadcast_to(1.0 / jnp.sqrt(squares / entries + 1e-06), (8, 128))
    sent("h")
    for c in stores:
        c.wait()


def finish(gath_hbm, coarse_hbm, scale_ref, coarse_out, kup_out, dup_out, eup_out, gin, kup, dup, eup, in_s, out_s):
    through = pltpu.make_async_copy(coarse_hbm, coarse_out, out_s.at[0])
    through.start()
    reads = []
    for u in range(8):
        c = pltpu.make_async_copy(gath_hbm.at[u], gin.at[u], in_s.at[u])
        c.start()
        reads.append(c)
    scale = scale_ref[0:1, :]
    writes = [through]

    def write(src, dst, index):
        c = pltpu.make_async_copy(src, dst, out_s.at[index])
        c.start()
        writes.append(c)

    for u in range(8):
        reads[u].wait()
        for p in range(4):
            block = 4 * u + p
            for e in range(2):
                lanes = slice(e * 128, (e + 1) * 128)
                if block == 31:
                    eup[:, lanes] = (gin[u, e, p, 0:64].astype(F32) * scale).astype(BF16)
                    continue
                v = (gin[u, e, p].astype(F32) * scale).astype(BF16)
                if block < 4:
                    dup[block, :, lanes] = v
                else:
                    kup[9 * (2 - (block - 4) // 9) + (block - 4) % 9, :, lanes] = v
            if block == 3:
                write(dup, dup_out, 1)
            elif block == 31:
                write(eup, eup_out, 2)
            elif block >= 4 and ((block - 4) % 9 == 8 or block % 4 == 3 or block == 30):
                since = max(4 * u, block - (block - 4) % 9)
                n = block - since + 1
                at = 9 * (2 - (block - 4) // 9) + (since - 4) % 9
                write(kup.at[pl.ds(at, n)], kup_out.at[pl.ds(at, n)], len(writes) + 2)
    for c in writes:
        c.wait()


def on_device(records, cell_ids, counts, embed, kernels, down, cotangent):
    vmem = pl.BlockSpec(memory_space=pltpu.VMEM)
    hbm = pl.BlockSpec(memory_space=pl.ANY)
    coarse, gath, scale = pl.pallas_call(
        body,
        out_shape=(
            jax.ShapeDtypeStruct((8, 24, 256), BF16),
            jax.ShapeDtypeStruct((8, 2, 4, 256, 128), BF16),
            jax.ShapeDtypeStruct((8, 128), F32),
        ),
        in_specs=[vmem, vmem, vmem, vmem, hbm, hbm, vmem],
        out_specs=(vmem, hbm, vmem),
        scratch_shapes=[
            pltpu.VMEM((3, 3, 3, 256, 256), BF16),
            pltpu.VMEM((2, 2, 256, 256), BF16),
            pltpu.VMEM((8, 16, 1152), BF16),
            pltpu.VMEM((8, 16, 1152), BF16),
            pltpu.VMEM((16, 16, 640), BF16),
            pltpu.VMEM((16, 16, 640), BF16),
            pltpu.VMEM((384, 2048), BF16),
            pltpu.VMEM((2048, 256), BF16),
            pltpu.VMEM((14, WIDE, 128), F32),
            pltpu.VMEM((12, 40, 256), F32),
            pltpu.VMEM((2, 12 * WIDE, 128), F32),
            pltpu.VMEM((2, 12 * WIDE, 128), F32),
            pltpu.VMEM((12, WIDE, 512), BF16),
            pltpu.VMEM((24, WIDE, 256), F32),
            pltpu.VMEM((3, ROWS, WIDE, 768), BF16),
            pltpu.VMEM((3, ROWS, WIDE, 256), F32),
            pltpu.VMEM((ROWS, WIDE, 768), BF16),
            pltpu.VMEM((18, WIDE, 768), BF16),
            pltpu.VMEM((256, 18 * WIDE), BF16),
            pltpu.VMEM((ROWS, WIDE, 256), BF16),
            pltpu.VMEM((2, 512, 128), F32),
                pltpu.VMEM((2, 32, 256, 128), BF16),
            pltpu.VMEM((32, 256, 128), BF16),
            pltpu.VMEM((32, 256, 128), BF16),
            pltpu.VMEM((8, 3, 256, 128), BF16),
            pltpu.VMEM((8, 256, 128), BF16),
            pltpu.VMEM((8, 15, 16, 128), BF16),
            pltpu.VMEM((8, 2, 4, 256, 128), BF16),
            pltpu.SemaphoreType.DMA((2,)),
            pltpu.SemaphoreType.DMA((7,)),
            pltpu.SemaphoreType.DMA((7,)),
            pltpu.SemaphoreType.DMA((15,)),
            pltpu.SemaphoreType.DMA((15,)),
            pltpu.SemaphoreType.DMA((2, 8)),
            pltpu.SemaphoreType.DMA((2, 8)),
            pltpu.SemaphoreType.DMA((301,)),
            pltpu.SemaphoreType.DMA((301,)),
            pltpu.SemaphoreType.DMA((8,)),
        ],
        compiler_params=pltpu.CompilerParams(
            collective_id=0, has_side_effects=True, vmem_limit_bytes=60 * 1024 * 1024
        ),
    )(records.reshape(128, 1024), jnp.swapaxes(cell_ids, 1, 2).reshape(16, 128), counts, embed, kernels, down, cotangent)
    coarse, kup, dup, eup = pl.pallas_call(
        finish,
        out_shape=(
            jax.ShapeDtypeStruct((8, 24, 256), BF16),
            jax.ShapeDtypeStruct((27, 256, 256), BF16),
            jax.ShapeDtypeStruct((4, 256, 256), BF16),
            jax.ShapeDtypeStruct((64, 256), BF16),
        ),
        in_specs=[hbm, hbm, vmem],
        out_specs=(hbm,) * 4,
        scratch_shapes=[
            pltpu.VMEM((8, 2, 4, 256, 128), BF16),
            pltpu.VMEM((27, 256, 256), BF16),
            pltpu.VMEM((4, 256, 256), BF16),
            pltpu.VMEM((64, 256), BF16),
            pltpu.SemaphoreType.DMA((8,)),
            pltpu.SemaphoreType.DMA((16,)),
        ],
        compiler_params=pltpu.CompilerParams(vmem_limit_bytes=60 * 1024 * 1024),
    )(gath, coarse, scale)
    return coarse, kup.reshape(3, 3, 3, 256, 256), dup.reshape(2, 2, 256, 256), eup


def solution(mesh):
    return jax.shard_map(
        on_device,
        mesh=mesh,
        in_specs=(
            P(("lat", "lon"), None, None),
            P(("lat", "lon"), None, None),
            P(("lat", "lon"), None),
            P(),
            P(),
            P(),
            P("lat", "lon", None),
        ),
        out_specs=(P("lat", "lon", None), P(), P(), P()),
        check_vma=False,
    )
```

```python
import jax
import jax.numpy as jnp
from jax import lax
from jax.experimental import pallas as pl
from jax.experimental.pallas import tpu as pltpu
from jax.sharding import PartitionSpec as P

F32 = jnp.float32
BF16 = jnp.bfloat16
MESH = pl.DeviceIdType.MESH

ROWS, WIDE = 28, 64
PIECES = ((0,), (1, 2), (3, 4), (5, 6), (7,))
PLANE = [(kb, kc) for kb in range(4) for kc in range(4) if (kb, kc) != (0, 0)]


def nn(a, b):
    return jnp.dot(a, b, preferred_element_type=F32)


def nt(a, b):
    return lax.dot_general(a, b, (((1,), (1,)), ((), ())), preferred_element_type=F32)


def body(
    records_hbm, ids_ref, counts_ref, embed_ref, kern_hbm, down_hbm, cot_hbm,
    coarse_ref, gath_hbm, scale_ref,
    kern_ref, down_ref, cot_ref, table, arr1, out2, in2,
    onehot, spread, mean, cpad, fine_e, fine_o, eo, up, x3, fac, dy3, dym, xt, xl, ybuf,
    grad, core_in, acc1, in1, acc2, in2r, gath,
    load_s, d1_s, d1_r, d2_s, d2_r, halo_s, halo_r, sum_s, sum_r, out_s,
):
    early = [
        pltpu.make_async_copy(records_hbm, table.at[:, :, pl.ds(0, 1024)], load_s.at[2]),
        pltpu.make_async_copy(cot_hbm, cot_ref, load_s.at[3]),
    ]
    for c in early:
        c.start()
    loads = [
        pltpu.make_async_copy(kern_hbm, kern_ref, load_s.at[0]),
        pltpu.make_async_copy(down_hbm, down_ref, load_s.at[1]),
    ]
    lat = lax.axis_index("lat")
    lon = lax.axis_index("lon")
    xx = lax.rem(lon // 2, 2) * 2 + lat // 4
    yy = lax.rem(lat, 4)
    zz = lon // 4
    core = lax.rem(lon, 2)
    pos = (xx, yy, zz)

    def by(offsets):
        c = [lax.rem(p + o, 4) for p, o in zip(pos, offsets)]
        return (lax.rem(c[0], 2) * 4 + c[1], c[2] * 4 + (c[0] // 2) * 2 + core)

    def along(axis, k):
        return by([k if i == axis else 0 for i in range(3)])

    def across(axis, kb, kc):
        b, c = (axis + 1) % 3, (axis + 2) % 3
        return by([kb if i == b else kc if i == c else 0 for i in range(3)])

    other = (lat, lon + 1 - 2 * core)

    def side(dr, dc):
        return (lax.rem(lat + dr + 8, 8), lax.rem(lon + dc + 16, 16))

    sides = [(r, c) for r in (-1, 0, 1) for c in (-1, 0, 1) if (r, c) != (0, 0)]
    partners = [by((dx, dy, 0)) for dx, dy in PLANE]
    partners += [by((0, dy, dz)) for dy in range(4) for dz in (1, 2, 3)]
    partners += [by((dx, 0, dz)) for dx in (1, 2, 3) for dz in (1, 2, 3)]
    partners += [(lat, lax.rem(lon + k, 16)) for k in range(1, 16, 2)]
    partners += [side(r, c) for r in (-1, 1) for c in (-1, 1)]
    barrier = pltpu.get_barrier_semaphore()
    for who in partners:
        pl.semaphore_signal(barrier, inc=1, device_id=who, device_id_type=MESH)

    cell = jnp.where(lax.broadcasted_iota(jnp.int32, (16, 128), 0) < counts_ref[...], ids_ref[...], 768)
    kk = lax.broadcasted_iota(jnp.int32, (128, 16), 1)
    ll = lax.broadcasted_iota(jnp.int32, (128, 16), 0)
    lane = (kk >> 3) * 16 + (kk & 7)
    digits = nn(jnp.where(ll == lane, 1.0, 0.0).astype(BF16), (cell >> 5).astype(F32).astype(BF16))
    digits = digits + nn(jnp.where(ll == lane + 8, 1.0, 0.0).astype(BF16), (cell & 31).astype(F32).astype(BF16))
    digits = digits.T
    for c in loads:
        c.start()
    for c in early:
        c.wait()
    table[:, :, 1024:1152] = digits.astype(BF16).reshape(8, 16, 128)
    cpad[2:10, 8:32, :] = cot_ref[...].astype(F32)
    pl.semaphore_wait(barrier, len(partners))

    def remote(src, dst, send_sem, recv_sem, who):
        c = pltpu.make_async_remote_copy(
            src_ref=src, dst_ref=dst, send_sem=send_sem, recv_sem=recv_sem, device_id=who, device_id_type=MESH
        )
        c.start()
        return c

    lat_copies = []
    for k in range(1, 8):
        p = lax.rem(lat + k, 8)
        lat_copies.append(remote(table.at[p], arr1.at[lat], d1_s.at[k - 1], d1_r.at[k - 1], (p, lon)))
    arr1[lat] = table[lat]
    for c in lat_copies:
        c.wait_recv()
    flat = arr1[...].reshape(128, 1152)
    rho = lax.broadcasted_iota(jnp.int32, (256, 128), 0)
    came = lax.broadcasted_iota(jnp.int32, (256, 128), 1)
    match = came == (rho & 7) * 16 + (rho >> 4)
    halves = [jnp.where(match & (((rho >> 3) & 1) == h), 1.0, 0.0).astype(BF16) for h in range(2)]
    second = pltpu.roll(flat[:, 1024:1152].astype(F32), 112, 1).astype(BF16)
    moved = nn(halves[0], flat[:, 0:512]) + nn(halves[1], flat[:, 512:1024])
    moved_ids = nn(halves[0], flat[:, 1024:1152]) + nn(halves[1], second)
    out2[:, :, 0:512] = moved.astype(BF16).reshape(16, 16, 512)
    out2[:, :, 512:640] = moved_ids.astype(BF16).reshape(16, 16, 128)
    lon_copies = []
    for k in range(1, 16):
        q = lax.rem(lon + k, 16)
        lon_copies.append(remote(out2.at[q], in2.at[lon], d2_s.at[k - 1], d2_r.at[k - 1], (lat, q)))
    in2[lon] = out2[lon]

    def span(step, rows, lead, cols, near):
        if step[0] == 0:
            r_src = r_dst = (lead, rows)
        elif step[0] < 0:
            r_src, r_dst = (lead, lead), (lead + rows, lead)
        else:
            r_src, r_dst = (rows, lead), (0, lead)
        if step[1] == 0:
            c_src = c_dst = (8, cols)
        elif step[1] < 0:
            c_src, c_dst = (8, 8), (8 + cols, 8)
        else:
            c_src, c_dst = (cols, 8), (0, 8)
        return r_src, c_src, r_dst, c_dst

    def halo(ref, rows, lead, cols, which):
        copies = []
        for n, step in enumerate(sides):
            (a, la), (b, lb), (c, lc), (d, ld) = span(step, rows, lead, cols, None)
            copies.append(
                pltpu.make_async_remote_copy(
                    src_ref=ref.at[pl.ds(a, la), pl.ds(b, lb), :],
                    dst_ref=ref.at[pl.ds(c, lc), pl.ds(d, ld), :],
                    send_sem=halo_s.at[which, n],
                    recv_sem=halo_r.at[which, n],
                    device_id=side(*step),
                    device_id_type=MESH,
                )
            )
        for c in copies:
            c.start()
        return copies

    cot_copies = halo(cpad, 8, 2, 24, 0)

    for c in lon_copies:
        c.wait_recv()
    code = in2[:, :, 512:640].reshape(256, 128).astype(F32)
    code = code * 32.0 + pltpu.roll(code, 120, 1)
    odds = (((code.astype(jnp.int32) * 1366) >> 16) & 1).astype(F32)
    idt = code.T[0:8].astype(jnp.int32)
    rowt = (idt * 1366) >> 16
    place = (rowt >> 1) * 48 + (idt - rowt * 48)
    cells = lax.broadcasted_iota(jnp.int32, (384, 256), 0)
    low = lax.broadcasted_iota(jnp.int32, (256, 128), 1) < 64
    for k in range(8):
        onehot[:, k * 256 : (k + 1) * 256] = jnp.where(cells == place[k : k + 1, :], 1.0, 0.0).astype(BF16)
        odd = odds[:, k : k + 1]
        flag = jnp.where(low, 1.0 - odd, odd)
        pair = in2[:, :, (k // 2) * 128 : (k // 2 + 1) * 128].reshape(256, 128).astype(F32)
        swap = pltpu.roll(pair, 64, 1)
        both = jnp.where(low, pair, swap) if k % 2 == 0 else jnp.where(low, swap, pair)
        spread[k * 256 : (k + 1) * 256, 0:128] = (both * flag).astype(BF16)
        spread[k * 256 : (k + 1) * 256, 128:256] = flag.astype(BF16)
    sums = nn(onehot[...], spread[...])
    means = (sums[:, 0:128] / jnp.maximum(sums[:, 128:256], 1.0)).astype(BF16).astype(F32)
    mean[3:11, 8:56, :] = means.reshape(8, 48, 128)
    mean_copies = halo(mean, 8, 3, 48, 1)

    for c in loads:
        c.wait()
    for c in cot_copies:
        c.wait_recv()
    fine_e[...] = jnp.zeros_like(fine_e)
    fine_o[...] = jnp.zeros_like(fine_o)
    coarse_cells = cpad[:, 4:36, :].reshape(384, 256)
    for h in range(2):
        part = coarse_cells[:, h * 128 : (h + 1) * 128]
        fine_e[h, pl.ds(0, 384, stride=2), :] = part
        fine_o[h, pl.ds(1, 384, stride=2), :] = part
    for h in range(2):
        eo[:, :, h * 128 : (h + 1) * 128] = fine_e[h].astype(BF16).reshape(12, WIDE, 128)
        eo[:, :, 256 + h * 128 : 256 + (h + 1) * 128] = fine_o[h].astype(BF16).reshape(12, WIDE, 128)
    for a in range(2):
        flat = eo[...].reshape(12 * WIDE, 512)
        top = nt(flat[:, 0:256], down_ref[a, 0]) + nt(flat[:, 256:512], down_ref[a, 1])
        top = top.reshape(12, WIDE, 256)
        for i in range(12):
            up[2 * i + a] = top[i]

    def inside(first, count):
        row = lax.broadcasted_iota(jnp.int32, (count, 1, 1), 0) + (lat * 16 - 6 + first)
        return jnp.where((row >= 0) & (row < 128), 1.0, 0.0)

    column = lax.broadcasted_iota(jnp.int32, (1, WIDE, 1), 1)
    in_tile = jnp.where((column >= 8) & (column < 56), 1.0, 0.0)

    def store3(ref, first, count, value, order):
        flat = value.reshape(count * WIDE, 256)
        prev = pltpu.roll(flat, 1, 0)
        nxt = pltpu.roll(flat, count * WIDE - 1, 0)
        parts = (prev, flat, nxt) if order > 0 else (nxt, flat, prev)
        for b, part in enumerate(parts):
            ref[first : first + count, :, b * 256 : (b + 1) * 256] = part.astype(BF16).reshape(count, WIDE, 256)

    def turn(ref_slice, count):
        return ref_slice.reshape(count * WIDE, 256).T

    for c in mean_copies:
        c.wait_recv()
    for first in (0, 7):
        lhs = mean[first : first + 7].reshape(7 * WIDE, 128).astype(BF16)
        zero = jnp.zeros((64, 256), BF16)
        for par in range(2):
            both = (embed_ref[...], zero) if par == 0 else (zero, embed_ref[...])
            x0 = nn(lhs, jnp.concatenate(both, 0)).reshape(7, WIDE, 256)
            row = lax.broadcasted_iota(jnp.int32, (7, 1, 1), 0) * 2 + (lat * 16 - 6 + 2 * first + par)
            x0 = x0 * jnp.where((row >= 0) & (row < 128), 1.0, 0.0)
            flat = x0.reshape(7 * WIDE, 256)
            parts = (pltpu.roll(flat, 1, 0), flat, pltpu.roll(flat, 7 * WIDE - 1, 0))
            for b, part in enumerate(parts):
                part = part.astype(BF16).reshape(7, WIDE, 256)
                for i in range(7):
                    x3[0, 2 * (first + i) + par, :, b * 256 : (b + 1) * 256] = part[i]

    for l in range(3):
        first, count = l + 1, 26 - 2 * l
        half = count // 2
        for start in (first, first + half):
            y = jnp.zeros((half * WIDE, 256), F32)
            for a in range(3):
                y = y + nn(
                    x3[l, start + a - 1 : start + a - 1 + half].reshape(half * WIDE, 768),
                    kern_ref[l, a].reshape(768, 256),
                )
            s = jax.nn.sigmoid(y)
            gain = (s * (1.0 + y * (1.0 - s))).reshape(half, WIDE, 256)
            keep = inside(start, half)
            fac[l, start : start + half] = gain * keep
            x = x3[l, start : start + half, :, 256:512].reshape(half * WIDE, 256).astype(F32)
            x = (x + y * s).reshape(half, WIDE, 256)
            if l < 2:
                store3(x3.at[l + 1], start, half, x * keep, 1)
            else:
                xl[start : start + half] = (x * in_tile).astype(BF16)

    last = xl[6:22].reshape(8, 2, WIDE, 256)
    rights = eo[2:10].reshape(512, 512)
    for a in range(2):
        g = nn(last[:, a].reshape(512, 256).T, rights).astype(BF16)
        for b in range(2):
            for e in range(2):
                grad[e, 2 * a + b] = g[:, b * 256 + e * 128 : b * 256 + (e + 1) * 128]

    def downsample():
        sum0 = jnp.zeros((512, 256), F32)
        sum1 = jnp.zeros((512, 256), F32)
        last = xl[6:22].reshape(8, 2, WIDE, 256)
        for a in range(2):
            piece = last[:, a].reshape(512, 256)
            sum0 = sum0 + nn(piece, down_ref[a, 0])
            sum1 = sum1 + nn(piece, down_ref[a, 1])
        total = sum0 + pltpu.roll(sum1, 511, 0)
        for h in range(2):
            ybuf[h] = total[:, h * 128 : (h + 1) * 128]
        for h in range(2):
            picked = ybuf[h, pl.ds(0, 256, stride=2), :].reshape(8, 32, 128)
            coarse_ref[:, :, h * 128 : (h + 1) * 128] = picked[:, 4:28].astype(BF16)

    stores = []
    owed = []

    def stage(kind, u):
        index = "abpgh".index(kind) * 8 + u
        return sum_s.at[index], sum_r.at[index]

    def arrive(sem, like):
        pltpu.make_async_copy(like, like, sem).wait()

    def rs_core(piece):
        b0, n = 4 * PIECES[piece][0], 4 * len(PIECES[piece])
        blocks = core_in.at[pl.ds(b0, n)]
        remote(grad.at[1 - core, pl.ds(b0, n)], blocks, sum_s.at[40 + piece], sum_r.at[40 + piece], other)
        owed.append((sum_s.at[40 + piece], blocks))

    def rs_axis(piece):
        arrive(sum_r.at[40 + piece], core_in.at[pl.ds(4 * PIECES[piece][0], 4 * len(PIECES[piece]))])
        for u in PIECES[piece]:
            for p in range(4):
                acc1[4 * u + p] = (grad[core, 4 * u + p].astype(F32) + core_in[4 * u + p].astype(F32)).astype(BF16)
            out, into = stage("a", u)
            for k in (1, 2, 3):
                p = lax.rem(pos[u % 3] + k, 4)
                remote(acc1.at[4 * u + p], in1.at[u, k - 1], out, into, along(u % 3, k))
            owed.append((out, in1.at[u]))

    def rs_plane(u):
        axis = u % 3
        arrive(stage("a", u)[1], in1.at[u])
        s = acc1[4 * u + pos[axis]].astype(F32)
        for k in range(3):
            s = s + in1[u, k].astype(F32)
        acc2[u] = s.astype(BF16)
        out, into = stage("b", u)
        for i, (kb, kc) in enumerate(PLANE):
            row = lax.rem(pos[(axis + 1) % 3] + kb, 4) * 64 + lax.rem(pos[(axis + 2) % 3] + kc, 4) * 16
            src = acc2.at[u, pl.ds(pl.multiple_of(row, 16), 16)]
            remote(src, in2r.at[u, i], out, into, across(axis, kb, kc))
        owed.append((out, in2r.at[u]))

    def ag_plane(u):
        axis = u % 3
        arrive(stage("b", u)[1], in2r.at[u])
        rows = pl.ds(pl.multiple_of(pos[(axis + 1) % 3] * 64 + pos[(axis + 2) % 3] * 16, 16), 16)
        s = acc2[u, rows, :].astype(F32)
        for i in range(15):
            s = s + in2r[u, i].astype(F32)
        part = gath.at[u, core, pos[axis], rows, :]
        gath[u, core, pos[axis], rows, :] = s.astype(BF16)
        out, into = stage("p", u)
        for kb, kc in PLANE:
            remote(part, part, out, into, across(axis, kb, kc))
        owed.append((out, in2r.at[u]))

    def ag_axis(u):
        axis = u % 3
        arrive(stage("p", u)[1], in2r.at[u])
        part = gath.at[u, core, pos[axis]]
        out, into = stage("g", u)
        for k in (1, 2, 3):
            remote(part, part, out, into, along(axis, k))
        owed.append((out, in1.at[u]))

    def ag_core(u):
        arrive(stage("g", u)[1], in1.at[u])
        part = gath.at[u, core]
        out, into = stage("h", u)
        remote(part, part, out, into, other)
        owed.append((out, part))

    def square(u):
        arrive(stage("h", u)[1], gath.at[u, core])
        c = pltpu.make_async_copy(gath.at[u], gath_hbm.at[u], out_s.at[u])
        c.start()
        stores.append(c)
        total = jnp.zeros((8, 128), F32)
        for e in range(2):
            for p in range(4):
                v = gath[u, e, p].astype(F32)
                total = total + jnp.sum((v * v).reshape(32, 8, 128), axis=0)
        return total

    def back(l):
        lo, count = 5 - l, 18 + 2 * l
        half = count // 2
        for start in (lo, lo + half):
            rows = slice(start - lo, start - lo + half)
            d = up[start - 2 : start - 2 + half] * fac[l, start : start + half]
            store3(dy3, start, half, d, -1)
        d = dy3[6:22, :, 256:512].astype(F32) * in_tile
        store3(dym, 1, 16, d, -1)

    def weights(l):
        xt[...] = turn(x3[l, 5:23, :, 256:512], 18)
        block = 4 + 9 * (2 - l)
        for a in range(3):
            if a == 1:
                g = nn(xt[...], dym[...].reshape(18 * WIDE, 768))
            else:
                g = nn(xt[:, 64 * a : 64 * a + 1024], dym[1:17].reshape(16 * WIDE, 768))
            g = g.astype(BF16)
            for b in range(3):
                for e in range(2):
                    grad[e, block + 3 * a + b] = g[:, b * 256 + e * 128 : b * 256 + (e + 1) * 128]

    def spread_back(l):
        lo, count = 6 - l, 16 + 2 * l
        half = count // 2
        for start in (lo, lo + half):
            d = jnp.zeros((half * WIDE, 256), F32)
            for a in range(3):
                for b in range(3):
                    src = dy3[start + 1 - a : start + 1 - a + half, :, b * 256 : (b + 1) * 256]
                    d = d + nt(src.reshape(half * WIDE, 256), kern_ref[l, a, b])
            here = slice(start - 2, start - 2 + half)
            up[here] = up[here] + d.reshape(half, WIDE, 256)

    zero_row = jnp.zeros((WIDE, 768), BF16)
    dym[0] = zero_row
    dym[17] = zero_row
    def each(step, piece):
        for u in PIECES[piece]:
            step(u)

    def sent(keep):
        while len(owed) > keep:
            arrive(*owed.pop(0))

    rs_core(0)
    back(2)
    rs_axis(0)
    weights(2)
    rs_core(1)
    spread_back(2)
    rs_axis(1)
    back(1)
    weights(1)
    rs_core(2)
    each(rs_plane, 0)
    spread_back(1)
    rs_axis(2)
    back(0)
    weights(0)
    rs_core(3)
    each(rs_plane, 1)
    spread_back(0)
    rs_axis(3)
    dx0 = (up[4:20] * in_tile).astype(BF16).reshape(8, 2, WIDE, 256)
    mt = mean[3:11].reshape(512, 128).T.astype(BF16)
    ge = nn(mt[0:64], dx0[:, 0].reshape(512, 256)) + nn(mt[64:128], dx0[:, 1].reshape(512, 256))
    for e in range(2):
        grad[e, 31] = jnp.zeros((256, 128), BF16)
        grad[e, 31, 0:64, :] = ge[:, e * 128 : (e + 1) * 128].astype(BF16)
    rs_core(4)
    each(ag_plane, 0)
    rs_axis(4)
    downsample()
    each(rs_plane, 2)
    each(ag_plane, 1)
    each(rs_plane, 3)
    each(ag_axis, 0)
    each(rs_plane, 4)
    each(ag_plane, 2)
    each(ag_axis, 1)
    each(ag_plane, 3)
    each(ag_plane, 4)
    each(ag_axis, 2)
    each(ag_core, 0)
    each(ag_axis, 3)
    each(ag_axis, 4)
    squares = square(0)
    each(ag_core, 1)
    for c in lat_copies + lon_copies + cot_copies + mean_copies:
        c.wait_send()
    sent(24)
    squares = squares + square(1) + square(2)
    each(ag_core, 2)
    sent(12)
    squares = squares + square(3) + square(4)
    each(ag_core, 3)
    squares = squares + square(5) + square(6)
    each(ag_core, 4)
    sent(1)
    squares = squares + square(7)
    entries = 31 * 65536 + 16384
    squares = jnp.sum(jnp.sum(squares, axis=0, keepdims=True), axis=1, keepdims=True)
    scale_ref[...] = jnp.broadcast_to(1.0 / jnp.sqrt(squares / entries + 1e-06), (8, 128))
    sent(0)
    for c in stores:
        c.wait()


def finish(gath_hbm, coarse_hbm, scale_ref, coarse_out, kup_out, dup_out, eup_out, gin, kup, dup, eup, in_s, out_s):
    through = pltpu.make_async_copy(coarse_hbm, coarse_out, out_s.at[0])
    through.start()
    reads = []
    for u in range(8):
        c = pltpu.make_async_copy(gath_hbm.at[u], gin.at[u], in_s.at[u])
        c.start()
        reads.append(c)
    scale = scale_ref[0:1, :]
    writes = [through]

    def write(src, dst, index):
        c = pltpu.make_async_copy(src, dst, out_s.at[index])
        c.start()
        writes.append(c)

    for u in range(8):
        reads[u].wait()
        for p in range(4):
            block = 4 * u + p
            for e in range(2):
                lanes = slice(e * 128, (e + 1) * 128)
                if block == 31:
                    eup[:, lanes] = (gin[u, e, p, 0:64].astype(F32) * scale).astype(BF16)
                    continue
                v = (gin[u, e, p].astype(F32) * scale).astype(BF16)
                if block < 4:
                    dup[block, :, lanes] = v
                else:
                    kup[9 * (2 - (block - 4) // 9) + (block - 4) % 9, :, lanes] = v
            if block == 3:
                write(dup, dup_out, 1)
            elif block == 31:
                write(eup, eup_out, 2)
            elif block >= 4 and ((block - 4) % 9 == 8 or block % 4 == 3 or block == 30):
                since = max(4 * u, block - (block - 4) % 9)
                n = block - since + 1
                at = 9 * (2 - (block - 4) // 9) + (since - 4) % 9
                write(kup.at[pl.ds(at, n)], kup_out.at[pl.ds(at, n)], len(writes) + 2)
    for c in writes:
        c.wait()


def on_device(records, cell_ids, counts, embed, kernels, down, cotangent):
    vmem = pl.BlockSpec(memory_space=pltpu.VMEM)
    hbm = pl.BlockSpec(memory_space=pl.ANY)
    coarse, gath, scale = pl.pallas_call(
        body,
        out_shape=(
            jax.ShapeDtypeStruct((8, 24, 256), BF16),
            jax.ShapeDtypeStruct((8, 2, 4, 256, 128), BF16),
            jax.ShapeDtypeStruct((8, 128), F32),
        ),
        in_specs=[hbm, vmem, vmem, vmem, hbm, hbm, hbm],
        out_specs=(vmem, hbm, vmem),
        scratch_shapes=[
            pltpu.VMEM((3, 3, 3, 256, 256), BF16),
            pltpu.VMEM((2, 2, 256, 256), BF16),
            pltpu.VMEM((8, 24, 256), BF16),
            pltpu.VMEM((8, 16, 1152), BF16),
            pltpu.VMEM((8, 16, 1152), BF16),
            pltpu.VMEM((16, 16, 640), BF16),
            pltpu.VMEM((16, 16, 640), BF16),
            pltpu.VMEM((384, 2048), BF16),
            pltpu.VMEM((2048, 256), BF16),
            pltpu.VMEM((14, WIDE, 128), F32),
            pltpu.VMEM((12, 40, 256), F32),
            pltpu.VMEM((2, 12 * WIDE, 128), F32),
            pltpu.VMEM((2, 12 * WIDE, 128), F32),
            pltpu.VMEM((12, WIDE, 512), BF16),
            pltpu.VMEM((24, WIDE, 256), F32),
            pltpu.VMEM((3, ROWS, WIDE, 768), BF16),
            pltpu.VMEM((3, ROWS, WIDE, 256), F32),
            pltpu.VMEM((ROWS, WIDE, 768), BF16),
            pltpu.VMEM((18, WIDE, 768), BF16),
            pltpu.VMEM((256, 18 * WIDE), BF16),
            pltpu.VMEM((ROWS, WIDE, 256), BF16),
            pltpu.VMEM((2, 512, 128), F32),
                pltpu.VMEM((2, 32, 256, 128), BF16),
            pltpu.VMEM((32, 256, 128), BF16),
            pltpu.VMEM((32, 256, 128), BF16),
            pltpu.VMEM((8, 3, 256, 128), BF16),
            pltpu.VMEM((8, 256, 128), BF16),
            pltpu.VMEM((8, 15, 16, 128), BF16),
            pltpu.VMEM((8, 2, 4, 256, 128), BF16),
            pltpu.SemaphoreType.DMA((4,)),
            pltpu.SemaphoreType.DMA((7,)),
            pltpu.SemaphoreType.DMA((7,)),
            pltpu.SemaphoreType.DMA((15,)),
            pltpu.SemaphoreType.DMA((15,)),
            pltpu.SemaphoreType.DMA((2, 8)),
            pltpu.SemaphoreType.DMA((2, 8)),
            pltpu.SemaphoreType.DMA((45,)),
            pltpu.SemaphoreType.DMA((45,)),
            pltpu.SemaphoreType.DMA((8,)),
        ],
        compiler_params=pltpu.CompilerParams(
            collective_id=0, has_side_effects=True, vmem_limit_bytes=60 * 1024 * 1024
        ),
    )(records.reshape(8, 16, 1024), jnp.swapaxes(cell_ids, 1, 2).reshape(16, 128), counts, embed, kernels, down, cotangent)
    coarse, kup, dup, eup = pl.pallas_call(
        finish,
        out_shape=(
            jax.ShapeDtypeStruct((8, 24, 256), BF16),
            jax.ShapeDtypeStruct((27, 256, 256), BF16),
            jax.ShapeDtypeStruct((4, 256, 256), BF16),
            jax.ShapeDtypeStruct((64, 256), BF16),
        ),
        in_specs=[hbm, hbm, vmem],
        out_specs=(hbm,) * 4,
        scratch_shapes=[
            pltpu.VMEM((8, 2, 4, 256, 128), BF16),
            pltpu.VMEM((27, 256, 256), BF16),
            pltpu.VMEM((4, 256, 256), BF16),
            pltpu.VMEM((64, 256), BF16),
            pltpu.SemaphoreType.DMA((8,)),
            pltpu.SemaphoreType.DMA((16,)),
        ],
        compiler_params=pltpu.CompilerParams(vmem_limit_bytes=60 * 1024 * 1024),
    )(gath, coarse, scale)
    return coarse, kup.reshape(3, 3, 3, 256, 256), dup.reshape(2, 2, 256, 256), eup


def solution(mesh):
    return jax.shard_map(
        on_device,
        mesh=mesh,
        in_specs=(
            P(("lat", "lon"), None, None),
            P(("lat", "lon"), None, None),
            P(("lat", "lon"), None),
            P(),
            P(),
            P(),
            P("lat", "lon", None),
        ),
        out_specs=(P("lat", "lon", None), P(), P(), P()),
        check_vma=False,
    )
```

```python
import jax
import jax.numpy as jnp
from jax import lax
from jax.experimental import pallas as pl
from jax.experimental.pallas import tpu as pltpu
from jax.sharding import PartitionSpec as P

F32 = jnp.float32
BF16 = jnp.bfloat16
MESH = pl.DeviceIdType.MESH

ROWS, WIDE = 28, 64
PIECES = ((0,), (1, 2), (3, 4), (5, 6), (7,))
PLANE = [(kb, kc) for kb in range(4) for kc in range(4) if (kb, kc) != (0, 0)]


def nn(a, b):
    return jnp.dot(a, b, preferred_element_type=F32)


def nt(a, b):
    return lax.dot_general(a, b, (((1,), (1,)), ((), ())), preferred_element_type=F32)


def body(
    records_hbm, ids_ref, counts_ref, embed_ref, kern_hbm, down_hbm, cot_hbm,
    coarse_ref, gath_hbm, scale_ref,
    kern_ref, down_ref, cot_ref, table, arr1, out2, in2,
    onehot, spread, mean, cpad, fine_e, fine_o, eo, up, x3, fac, dy3, dym, xt, xl, ybuf,
    grad, core_in, acc1, in1, acc2, in2r, gath,
    load_s, d_s, d_r, halo_s, halo_r, sum_s, sum_r, out_s,
):
    early = [
        pltpu.make_async_copy(records_hbm, table.at[:, :, pl.ds(0, 1024)], load_s.at[2]),
        pltpu.make_async_copy(cot_hbm, cot_ref, load_s.at[3]),
    ]
    for c in early:
        c.start()
    loads = [
        pltpu.make_async_copy(kern_hbm, kern_ref, load_s.at[0]),
        pltpu.make_async_copy(down_hbm, down_ref, load_s.at[1]),
    ]
    lat = lax.axis_index("lat")
    lon = lax.axis_index("lon")
    xx = lax.rem(lon // 2, 2) * 2 + lat // 4
    yy = lax.rem(lat, 4)
    zz = lon // 4
    core = lax.rem(lon, 2)
    pos = (xx, yy, zz)

    def by(offsets):
        c = [lax.rem(p + o, 4) for p, o in zip(pos, offsets)]
        return (lax.rem(c[0], 2) * 4 + c[1], c[2] * 4 + (c[0] // 2) * 2 + core)

    def along(axis, k):
        return by([k if i == axis else 0 for i in range(3)])

    def across(axis, kb, kc):
        b, c = (axis + 1) % 3, (axis + 2) % 3
        return by([kb if i == b else kc if i == c else 0 for i in range(3)])

    other = (lat, lon + 1 - 2 * core)

    def side(dr, dc):
        return (lax.rem(lat + dr + 8, 8), lax.rem(lon + dc + 16, 16))

    sides = [(r, c) for r in (-1, 0, 1) for c in (-1, 0, 1) if (r, c) != (0, 0)]
    partners = [by((dx, dy, 0)) for dx, dy in PLANE]
    partners += [by((0, dy, dz)) for dy in range(4) for dz in (1, 2, 3)]
    partners += [by((dx, 0, dz)) for dx in (1, 2, 3) for dz in (1, 2, 3)]
    partners += [(lat, lax.rem(lon + k, 16)) for k in range(1, 16, 2)]
    partners += [side(r, c) for r in (-1, 1) for c in (-1, 1)]
    barrier = pltpu.get_barrier_semaphore()
    for who in partners:
        pl.semaphore_signal(barrier, inc=1, device_id=who, device_id_type=MESH)

    cell = jnp.where(lax.broadcasted_iota(jnp.int32, (16, 128), 0) < counts_ref[...], ids_ref[...], 768)
    kk = lax.broadcasted_iota(jnp.int32, (128, 16), 1)
    ll = lax.broadcasted_iota(jnp.int32, (128, 16), 0)
    lane = (kk >> 3) * 16 + (kk & 7)
    digits = nn(jnp.where(ll == lane, 1.0, 0.0).astype(BF16), (cell >> 5).astype(F32).astype(BF16))
    digits = digits + nn(jnp.where(ll == lane + 8, 1.0, 0.0).astype(BF16), (cell & 31).astype(F32).astype(BF16))
    digits = digits.T
    for c in loads:
        c.start()
    for c in early:
        c.wait()
    table[:, :, 1024:1152] = digits.astype(BF16).reshape(8, 16, 128)
    cpad[2:10, 8:32, :] = cot_ref[...].astype(F32)
    pl.semaphore_wait(barrier, len(partners))

    def remote(src, dst, send_sem, recv_sem, who):
        c = pltpu.make_async_remote_copy(
            src_ref=src, dst_ref=dst, send_sem=send_sem, recv_sem=recv_sem, device_id=who, device_id_type=MESH
        )
        c.start()
        return c

    def arrive(sem, like):
        pltpu.make_async_copy(like, like, sem).wait()

    for k in range(1, 8):
        p = lax.rem(lat + k, 8)
        remote(table.at[p], arr1.at[lat], d_s.at[0], d_r.at[0], (p, lon))
    arr1[lat] = table[lat]
    arrive(d_r.at[0], arr1.at[pl.ds(0, 7)])
    flat = arr1[...].reshape(128, 1152)
    rho = lax.broadcasted_iota(jnp.int32, (256, 128), 0)
    came = lax.broadcasted_iota(jnp.int32, (256, 128), 1)
    match = came == (rho & 7) * 16 + (rho >> 4)
    halves = [jnp.where(match & (((rho >> 3) & 1) == h), 1.0, 0.0).astype(BF16) for h in range(2)]
    second = pltpu.roll(flat[:, 1024:1152].astype(F32), 112, 1).astype(BF16)
    moved = nn(halves[0], flat[:, 0:512]) + nn(halves[1], flat[:, 512:1024])
    moved_ids = nn(halves[0], flat[:, 1024:1152]) + nn(halves[1], second)
    out2[:, :, 0:512] = moved.astype(BF16).reshape(16, 16, 512)
    out2[:, :, 512:640] = moved_ids.astype(BF16).reshape(16, 16, 128)
    for k in range(1, 16):
        q = lax.rem(lon + k, 16)
        remote(out2.at[q], in2.at[lon], d_s.at[1], d_r.at[1], (lat, q))
    in2[lon] = out2[lon]

    def span(step, rows, lead, cols, near):
        if step[0] == 0:
            r_src = r_dst = (lead, rows)
        elif step[0] < 0:
            r_src, r_dst = (lead, lead), (lead + rows, lead)
        else:
            r_src, r_dst = (rows, lead), (0, lead)
        if step[1] == 0:
            c_src = c_dst = (8, cols)
        elif step[1] < 0:
            c_src, c_dst = (8, 8), (8 + cols, 8)
        else:
            c_src, c_dst = (cols, 8), (0, 8)
        return r_src, c_src, r_dst, c_dst

    def halo(ref, rows, lead, cols, which):
        copies = []
        for n, step in enumerate(sides):
            (a, la), (b, lb), (c, lc), (d, ld) = span(step, rows, lead, cols, None)
            copies.append(
                pltpu.make_async_remote_copy(
                    src_ref=ref.at[pl.ds(a, la), pl.ds(b, lb), :],
                    dst_ref=ref.at[pl.ds(c, lc), pl.ds(d, ld), :],
                    send_sem=halo_s.at[which, n],
                    recv_sem=halo_r.at[which, n],
                    device_id=side(*step),
                    device_id_type=MESH,
                )
            )
        for c in copies:
            c.start()
        return copies

    cot_copies = halo(cpad, 8, 2, 24, 0)

    arrive(d_r.at[1], in2.at[pl.ds(0, 15)])
    code = in2[:, :, 512:640].reshape(256, 128).astype(F32)
    code = code * 32.0 + pltpu.roll(code, 120, 1)
    odds = (((code.astype(jnp.int32) * 1366) >> 16) & 1).astype(F32)
    idt = code.T[0:8].astype(jnp.int32)
    rowt = (idt * 1366) >> 16
    place = (rowt >> 1) * 48 + (idt - rowt * 48)
    cells = lax.broadcasted_iota(jnp.int32, (384, 256), 0)
    low = lax.broadcasted_iota(jnp.int32, (256, 128), 1) < 64
    for k in range(8):
        onehot[:, k * 256 : (k + 1) * 256] = jnp.where(cells == place[k : k + 1, :], 1.0, 0.0).astype(BF16)
        odd = odds[:, k : k + 1]
        flag = jnp.where(low, 1.0 - odd, odd)
        pair = in2[:, :, (k // 2) * 128 : (k // 2 + 1) * 128].reshape(256, 128).astype(F32)
        swap = pltpu.roll(pair, 64, 1)
        both = jnp.where(low, pair, swap) if k % 2 == 0 else jnp.where(low, swap, pair)
        spread[k * 256 : (k + 1) * 256, 0:128] = (both * flag).astype(BF16)
        spread[k * 256 : (k + 1) * 256, 128:256] = flag.astype(BF16)
    sums = nn(onehot[...], spread[...])
    means = (sums[:, 0:128] / jnp.maximum(sums[:, 128:256], 1.0)).astype(BF16).astype(F32)
    mean[3:11, 8:56, :] = means.reshape(8, 48, 128)
    mean_copies = halo(mean, 8, 3, 48, 1)

    for c in loads:
        c.wait()
    for c in cot_copies:
        c.wait_recv()
    fine_e[...] = jnp.zeros_like(fine_e)
    fine_o[...] = jnp.zeros_like(fine_o)
    coarse_cells = cpad[:, 4:36, :].reshape(384, 256)
    for h in range(2):
        part = coarse_cells[:, h * 128 : (h + 1) * 128]
        fine_e[h, pl.ds(0, 384, stride=2), :] = part
        fine_o[h, pl.ds(1, 384, stride=2), :] = part
    for h in range(2):
        eo[:, :, h * 128 : (h + 1) * 128] = fine_e[h].astype(BF16).reshape(12, WIDE, 128)
        eo[:, :, 256 + h * 128 : 256 + (h + 1) * 128] = fine_o[h].astype(BF16).reshape(12, WIDE, 128)
    for a in range(2):
        flat = eo[...].reshape(12 * WIDE, 512)
        top = nt(flat[:, 0:256], down_ref[a, 0]) + nt(flat[:, 256:512], down_ref[a, 1])
        top = top.reshape(12, WIDE, 256)
        for i in range(12):
            up[2 * i + a] = top[i]

    def inside(first, count):
        row = lax.broadcasted_iota(jnp.int32, (count, 1, 1), 0) + (lat * 16 - 6 + first)
        return jnp.where((row >= 0) & (row < 128), 1.0, 0.0)

    column = lax.broadcasted_iota(jnp.int32, (1, WIDE, 1), 1)
    in_tile = jnp.where((column >= 8) & (column < 56), 1.0, 0.0)

    def store3(ref, first, count, value, order):
        flat = value.reshape(count * WIDE, 256)
        prev = pltpu.roll(flat, 1, 0)
        nxt = pltpu.roll(flat, count * WIDE - 1, 0)
        parts = (prev, flat, nxt) if order > 0 else (nxt, flat, prev)
        for b, part in enumerate(parts):
            ref[first : first + count, :, b * 256 : (b + 1) * 256] = part.astype(BF16).reshape(count, WIDE, 256)

    def turn(ref_slice, count):
        return ref_slice.reshape(count * WIDE, 256).T

    for c in mean_copies:
        c.wait_recv()
    for first in (0, 7):
        lhs = mean[first : first + 7].reshape(7 * WIDE, 128).astype(BF16)
        zero = jnp.zeros((64, 256), BF16)
        for par in range(2):
            both = (embed_ref[...], zero) if par == 0 else (zero, embed_ref[...])
            x0 = nn(lhs, jnp.concatenate(both, 0)).reshape(7, WIDE, 256)
            row = lax.broadcasted_iota(jnp.int32, (7, 1, 1), 0) * 2 + (lat * 16 - 6 + 2 * first + par)
            x0 = x0 * jnp.where((row >= 0) & (row < 128), 1.0, 0.0)
            flat = x0.reshape(7 * WIDE, 256)
            parts = (pltpu.roll(flat, 1, 0), flat, pltpu.roll(flat, 7 * WIDE - 1, 0))
            for b, part in enumerate(parts):
                part = part.astype(BF16).reshape(7, WIDE, 256)
                for i in range(7):
                    x3[0, 2 * (first + i) + par, :, b * 256 : (b + 1) * 256] = part[i]

    for l in range(3):
        first, count = l + 1, 26 - 2 * l
        half = count // 2
        for start in (first, first + half):
            y = jnp.zeros((half * WIDE, 256), F32)
            for a in range(3):
                y = y + nn(
                    x3[l, start + a - 1 : start + a - 1 + half].reshape(half * WIDE, 768),
                    kern_ref[l, a].reshape(768, 256),
                )
            s = jax.nn.sigmoid(y)
            gain = (s * (1.0 + y * (1.0 - s))).reshape(half, WIDE, 256)
            keep = inside(start, half)
            fac[l, start : start + half] = gain * keep
            x = x3[l, start : start + half, :, 256:512].reshape(half * WIDE, 256).astype(F32)
            x = (x + y * s).reshape(half, WIDE, 256)
            if l < 2:
                store3(x3.at[l + 1], start, half, x * keep, 1)
            else:
                xl[start : start + half] = (x * in_tile).astype(BF16)

    last = xl[6:22].reshape(8, 2, WIDE, 256)
    rights = eo[2:10].reshape(512, 512)
    for a in range(2):
        g = nn(last[:, a].reshape(512, 256).T, rights).astype(BF16)
        for b in range(2):
            for e in range(2):
                grad[e, 2 * a + b] = g[:, b * 256 + e * 128 : b * 256 + (e + 1) * 128]

    def downsample():
        sum0 = jnp.zeros((512, 256), F32)
        sum1 = jnp.zeros((512, 256), F32)
        last = xl[6:22].reshape(8, 2, WIDE, 256)
        for a in range(2):
            piece = last[:, a].reshape(512, 256)
            sum0 = sum0 + nn(piece, down_ref[a, 0])
            sum1 = sum1 + nn(piece, down_ref[a, 1])
        total = sum0 + pltpu.roll(sum1, 511, 0)
        for h in range(2):
            ybuf[h] = total[:, h * 128 : (h + 1) * 128]
        for h in range(2):
            picked = ybuf[h, pl.ds(0, 256, stride=2), :].reshape(8, 32, 128)
            coarse_ref[:, :, h * 128 : (h + 1) * 128] = picked[:, 4:28].astype(BF16)

    stores = []
    owed = []

    def stage(kind, u):
        index = "abpgh".index(kind) * 8 + u
        return sum_s.at[index], sum_r.at[index]

    def rs_core(piece):
        b0, n = 4 * PIECES[piece][0], 4 * len(PIECES[piece])
        blocks = core_in.at[pl.ds(b0, n)]
        remote(grad.at[1 - core, pl.ds(b0, n)], blocks, sum_s.at[40 + piece], sum_r.at[40 + piece], other)
        owed.append((sum_s.at[40 + piece], blocks))

    def rs_axis(piece):
        arrive(sum_r.at[40 + piece], core_in.at[pl.ds(4 * PIECES[piece][0], 4 * len(PIECES[piece]))])
        for u in PIECES[piece]:
            for p in range(4):
                acc1[4 * u + p] = (grad[core, 4 * u + p].astype(F32) + core_in[4 * u + p].astype(F32)).astype(BF16)
            out, into = stage("a", u)
            for k in (1, 2, 3):
                p = lax.rem(pos[u % 3] + k, 4)
                remote(acc1.at[4 * u + p], in1.at[u, k - 1], out, into, along(u % 3, k))
            owed.append((out, in1.at[u]))

    def rs_plane(u):
        axis = u % 3
        arrive(stage("a", u)[1], in1.at[u])
        s = acc1[4 * u + pos[axis]].astype(F32)
        for k in range(3):
            s = s + in1[u, k].astype(F32)
        acc2[u] = s.astype(BF16)
        out, into = stage("b", u)
        for i, (kb, kc) in enumerate(PLANE):
            row = lax.rem(pos[(axis + 1) % 3] + kb, 4) * 64 + lax.rem(pos[(axis + 2) % 3] + kc, 4) * 16
            src = acc2.at[u, pl.ds(pl.multiple_of(row, 16), 16)]
            remote(src, in2r.at[u, i], out, into, across(axis, kb, kc))
        owed.append((out, in2r.at[u]))

    def ag_plane(u):
        axis = u % 3
        arrive(stage("b", u)[1], in2r.at[u])
        rows = pl.ds(pl.multiple_of(pos[(axis + 1) % 3] * 64 + pos[(axis + 2) % 3] * 16, 16), 16)
        s = acc2[u, rows, :].astype(F32)
        for i in range(15):
            s = s + in2r[u, i].astype(F32)
        part = gath.at[u, core, pos[axis], rows, :]
        gath[u, core, pos[axis], rows, :] = s.astype(BF16)
        out, into = stage("p", u)
        for kb, kc in PLANE:
            remote(part, part, out, into, across(axis, kb, kc))
        owed.append((out, in2r.at[u]))

    def ag_axis(u):
        axis = u % 3
        arrive(stage("p", u)[1], in2r.at[u])
        part = gath.at[u, core, pos[axis]]
        out, into = stage("g", u)
        for k in (1, 2, 3):
            remote(part, part, out, into, along(axis, k))
        owed.append((out, in1.at[u]))

    def ag_core(u):
        arrive(stage("g", u)[1], in1.at[u])
        part = gath.at[u, core]
        out, into = stage("h", u)
        remote(part, part, out, into, other)
        owed.append((out, part))

    def square(u):
        arrive(stage("h", u)[1], gath.at[u, core])
        c = pltpu.make_async_copy(gath.at[u], gath_hbm.at[u], out_s.at[u])
        c.start()
        stores.append(c)
        total = jnp.zeros((8, 128), F32)
        for e in range(2):
            for p in range(4):
                v = gath[u, e, p].astype(F32)
                total = total + jnp.sum((v * v).reshape(32, 8, 128), axis=0)
        return total

    def back(l):
        lo, count = 5 - l, 18 + 2 * l
        half = count // 2
        for start in (lo, lo + half):
            rows = slice(start - lo, start - lo + half)
            d = up[start - 2 : start - 2 + half] * fac[l, start : start + half]
            store3(dy3, start, half, d, -1)
        d = dy3[6:22, :, 256:512].astype(F32) * in_tile
        store3(dym, 1, 16, d, -1)

    def weights(l):
        xt[...] = turn(x3[l, 5:23, :, 256:512], 18)
        block = 4 + 9 * (2 - l)
        for a in range(3):
            if a == 1:
                g = nn(xt[...], dym[...].reshape(18 * WIDE, 768))
            else:
                g = nn(xt[:, 64 * a : 64 * a + 1024], dym[1:17].reshape(16 * WIDE, 768))
            g = g.astype(BF16)
            for b in range(3):
                for e in range(2):
                    grad[e, block + 3 * a + b] = g[:, b * 256 + e * 128 : b * 256 + (e + 1) * 128]

    def spread_back(l):
        lo, count = 6 - l, 16 + 2 * l
        half = count // 2
        for start in (lo, lo + half):
            d = jnp.zeros((half * WIDE, 256), F32)
            for a in range(3):
                for b in range(3):
                    src = dy3[start + 1 - a : start + 1 - a + half, :, b * 256 : (b + 1) * 256]
                    d = d + nt(src.reshape(half * WIDE, 256), kern_ref[l, a, b])
            here = slice(start - 2, start - 2 + half)
            up[here] = up[here] + d.reshape(half, WIDE, 256)

    zero_row = jnp.zeros((WIDE, 768), BF16)
    dym[0] = zero_row
    dym[17] = zero_row
    def each(step, piece):
        for u in PIECES[piece]:
            step(u)

    def sent(keep):
        while len(owed) > keep:
            arrive(*owed.pop(0))

    rs_core(0)
    back(2)
    rs_axis(0)
    weights(2)
    rs_core(1)
    spread_back(2)
    rs_axis(1)
    back(1)
    weights(1)
    rs_core(2)
    each(rs_plane, 0)
    spread_back(1)
    rs_axis(2)
    back(0)
    weights(0)
    rs_core(3)
    each(rs_plane, 1)
    spread_back(0)
    rs_axis(3)
    dx0 = (up[4:20] * in_tile).astype(BF16).reshape(8, 2, WIDE, 256)
    mt = mean[3:11].reshape(512, 128).T.astype(BF16)
    ge = nn(mt[0:64], dx0[:, 0].reshape(512, 256)) + nn(mt[64:128], dx0[:, 1].reshape(512, 256))
    for e in range(2):
        grad[e, 31] = jnp.zeros((256, 128), BF16)
        grad[e, 31, 0:64, :] = ge[:, e * 128 : (e + 1) * 128].astype(BF16)
    rs_core(4)
    each(ag_plane, 0)
    rs_axis(4)
    downsample()
    each(rs_plane, 2)
    each(ag_plane, 1)
    each(rs_plane, 3)
    each(ag_axis, 0)
    each(rs_plane, 4)
    each(ag_plane, 2)
    each(ag_axis, 1)
    each(ag_plane, 3)
    each(ag_plane, 4)
    each(ag_axis, 2)
    each(ag_core, 0)
    each(ag_axis, 3)
    each(ag_axis, 4)
    squares = square(0)
    each(ag_core, 1)
    arrive(d_s.at[0], arr1.at[pl.ds(0, 7)])
    arrive(d_s.at[1], in2.at[pl.ds(0, 15)])
    for c in cot_copies + mean_copies:
        c.wait_send()
    sent(24)
    squares = squares + square(1) + square(2)
    each(ag_core, 2)
    sent(12)
    squares = squares + square(3) + square(4)
    each(ag_core, 3)
    squares = squares + square(5) + square(6)
    each(ag_core, 4)
    sent(1)
    squares = squares + square(7)
    entries = 31 * 65536 + 16384
    squares = jnp.sum(jnp.sum(squares, axis=0, keepdims=True), axis=1, keepdims=True)
    scale_ref[...] = jnp.broadcast_to(1.0 / jnp.sqrt(squares / entries + 1e-06), (8, 128))
    sent(0)
    for c in stores:
        c.wait()


def finish(gath_hbm, coarse_hbm, scale_ref, coarse_out, kup_out, dup_out, eup_out, gin, kup, dup, eup, in_s, out_s):
    through = pltpu.make_async_copy(coarse_hbm, coarse_out, out_s.at[0])
    through.start()
    reads = []
    for u in range(8):
        c = pltpu.make_async_copy(gath_hbm.at[u], gin.at[u], in_s.at[u])
        c.start()
        reads.append(c)
    scale = scale_ref[0:1, :]
    writes = [through]

    def write(src, dst, index):
        c = pltpu.make_async_copy(src, dst, out_s.at[index])
        c.start()
        writes.append(c)

    for u in range(8):
        reads[u].wait()
        for p in range(4):
            block = 4 * u + p
            for e in range(2):
                lanes = slice(e * 128, (e + 1) * 128)
                if block == 31:
                    eup[:, lanes] = (gin[u, e, p, 0:64].astype(F32) * scale).astype(BF16)
                    continue
                v = (gin[u, e, p].astype(F32) * scale).astype(BF16)
                if block < 4:
                    dup[block, :, lanes] = v
                else:
                    kup[9 * (2 - (block - 4) // 9) + (block - 4) % 9, :, lanes] = v
            if block == 3:
                write(dup, dup_out, 1)
            elif block == 31:
                write(eup, eup_out, 2)
            elif block >= 4 and ((block - 4) % 9 == 8 or block % 4 == 3 or block == 30):
                since = max(4 * u, block - (block - 4) % 9)
                n = block - since + 1
                at = 9 * (2 - (block - 4) // 9) + (since - 4) % 9
                write(kup.at[pl.ds(at, n)], kup_out.at[pl.ds(at, n)], len(writes) + 2)
    for c in writes:
        c.wait()


def on_device(records, cell_ids, counts, embed, kernels, down, cotangent):
    vmem = pl.BlockSpec(memory_space=pltpu.VMEM)
    hbm = pl.BlockSpec(memory_space=pl.ANY)
    coarse, gath, scale = pl.pallas_call(
        body,
        out_shape=(
            jax.ShapeDtypeStruct((8, 24, 256), BF16),
            jax.ShapeDtypeStruct((8, 2, 4, 256, 128), BF16),
            jax.ShapeDtypeStruct((8, 128), F32),
        ),
        in_specs=[hbm, vmem, vmem, vmem, hbm, hbm, hbm],
        out_specs=(vmem, hbm, vmem),
        scratch_shapes=[
            pltpu.VMEM((3, 3, 3, 256, 256), BF16),
            pltpu.VMEM((2, 2, 256, 256), BF16),
            pltpu.VMEM((8, 24, 256), BF16),
            pltpu.VMEM((8, 16, 1152), BF16),
            pltpu.VMEM((8, 16, 1152), BF16),
            pltpu.VMEM((16, 16, 640), BF16),
            pltpu.VMEM((16, 16, 640), BF16),
            pltpu.VMEM((384, 2048), BF16),
            pltpu.VMEM((2048, 256), BF16),
            pltpu.VMEM((14, WIDE, 128), F32),
            pltpu.VMEM((12, 40, 256), F32),
            pltpu.VMEM((2, 12 * WIDE, 128), F32),
            pltpu.VMEM((2, 12 * WIDE, 128), F32),
            pltpu.VMEM((12, WIDE, 512), BF16),
            pltpu.VMEM((24, WIDE, 256), F32),
            pltpu.VMEM((3, ROWS, WIDE, 768), BF16),
            pltpu.VMEM((3, ROWS, WIDE, 256), F32),
            pltpu.VMEM((ROWS, WIDE, 768), BF16),
            pltpu.VMEM((18, WIDE, 768), BF16),
            pltpu.VMEM((256, 18 * WIDE), BF16),
            pltpu.VMEM((ROWS, WIDE, 256), BF16),
            pltpu.VMEM((2, 512, 128), F32),
                pltpu.VMEM((2, 32, 256, 128), BF16),
            pltpu.VMEM((32, 256, 128), BF16),
            pltpu.VMEM((32, 256, 128), BF16),
            pltpu.VMEM((8, 3, 256, 128), BF16),
            pltpu.VMEM((8, 256, 128), BF16),
            pltpu.VMEM((8, 15, 16, 128), BF16),
            pltpu.VMEM((8, 2, 4, 256, 128), BF16),
            pltpu.SemaphoreType.DMA((4,)),
            pltpu.SemaphoreType.DMA((2,)),
            pltpu.SemaphoreType.DMA((2,)),
            pltpu.SemaphoreType.DMA((2, 8)),
            pltpu.SemaphoreType.DMA((2, 8)),
            pltpu.SemaphoreType.DMA((45,)),
            pltpu.SemaphoreType.DMA((45,)),
            pltpu.SemaphoreType.DMA((8,)),
        ],
        compiler_params=pltpu.CompilerParams(
            collective_id=0, has_side_effects=True, vmem_limit_bytes=60 * 1024 * 1024
        ),
    )(records.reshape(8, 16, 1024), jnp.swapaxes(cell_ids, 1, 2).reshape(16, 128), counts, embed, kernels, down, cotangent)
    coarse, kup, dup, eup = pl.pallas_call(
        finish,
        out_shape=(
            jax.ShapeDtypeStruct((8, 24, 256), BF16),
            jax.ShapeDtypeStruct((27, 256, 256), BF16),
            jax.ShapeDtypeStruct((4, 256, 256), BF16),
            jax.ShapeDtypeStruct((64, 256), BF16),
        ),
        in_specs=[hbm, hbm, vmem],
        out_specs=(hbm,) * 4,
        scratch_shapes=[
            pltpu.VMEM((8, 2, 4, 256, 128), BF16),
            pltpu.VMEM((27, 256, 256), BF16),
            pltpu.VMEM((4, 256, 256), BF16),
            pltpu.VMEM((64, 256), BF16),
            pltpu.SemaphoreType.DMA((8,)),
            pltpu.SemaphoreType.DMA((16,)),
        ],
        compiler_params=pltpu.CompilerParams(vmem_limit_bytes=60 * 1024 * 1024),
    )(gath, coarse, scale)
    return coarse, kup.reshape(3, 3, 3, 256, 256), dup.reshape(2, 2, 256, 256), eup


def solution(mesh):
    return jax.shard_map(
        on_device,
        mesh=mesh,
        in_specs=(
            P(("lat", "lon"), None, None),
            P(("lat", "lon"), None, None),
            P(("lat", "lon"), None),
            P(),
            P(),
            P(),
            P("lat", "lon", None),
        ),
        out_specs=(P("lat", "lon", None), P(), P(), P()),
        check_vma=False,
    )
```
